256 devices in a mesh: band: 32 (over z, x_lo, core), slab: 8 (over x_hi, y).
Axes of the slice: x: 4 (x_hi: 2, x_lo: 2; x = x_hi * 2 + x_lo), y: 4, z: 8, core: 2. Of those that a mesh axis runs over, the one named last changes fastest.
Arguments:
- orbitals: float32 [128, 96, 4608], P('band', 'slab'), may hold values from -3 to 3
- owner: int32 [2], replicated, may hold values from 0 to 31
- picks: int32 [2, 2], replicated, may hold values from 0 to 3
Outputs:
- exchange_field: float32 [128, 96, 4608], P('band', 'slab')
- transposed: float32 [2, 2, 96, 4608], P(None, None, 'slab')
The draws below stay inside these ranges and needn't reach their ends.
Inputs may be any that keep to these rules, and one draw needn't show every extreme that they name: owner names a band group and picks positions within it; the two picks of a step may coincide.
All inputs are finite; a program needn't handle non-finite values.
Results may differ from the reference program's by a relative error of at most 0.0001.
Values sent between devices are 32-bit elements; how exact they have to be, the bound alone decides.
No kernel may reach another device: no remote copies, remote signals or barrier semaphores. Data moves between devices by JAX's collectives and lax.ppermute only.
A program may use at most 128 MiB of HBM per device.

```python
import math
import jax
import jax.numpy as jnp
from jax import lax

NX = 48
NY = 96
NZ = 96
BLOC = 4
STEPS = 2
BANDS = 128
N_BAND = 32


def touch_ends(array, own_key, least, largest):
    longest = array.shape.index(max(array.shape))
    spots = []
    for shift in (0, 1):
        where = [jax.random.randint(jax.random.fold_in(own_key, axis), (), 0, length) for axis, length in enumerate(array.shape)]
        where[longest] = (where[longest] + shift) % array.shape[longest]
        spots.append(tuple(where))
    return array.at[spots[0]].set(least).at[spots[1]].set(largest)


def block_levels(rng, extent, shards, low, top_value):
    gain, own = 1.0, jax.random.fold_in(rng, 6)
    for axis_at, blocks in shards:
        heights = jnp.exp(jax.random.uniform(jax.random.fold_in(own, axis_at), (blocks,), jnp.float32, low / len(shards), top_value / len(shards)))
        gain = gain * jnp.repeat(heights, extent[axis_at] // blocks).reshape([-1 if axis == axis_at else 1 for axis in range(len(extent))])
    return gain


def noise(own_key, extent, deviation, limit, shards=(), kind=jnp.bfloat16):
    array = deviation * jax.random.normal(own_key, extent, jnp.float32)
    if shards:
        array = array * block_levels(own_key, extent, shards, -0.22, 0.18)
    return jnp.clip(array, -limit, limit).astype(kind)


def setup_inputs(seed: int = 0) -> dict:
    seeds = jax.random.split(jax.random.key(seed), 4)
    orbitals = noise(seeds[0], (BANDS, NZ, NY * NX), 0.5, 3.0, ((0, 32), (1, 8)), jnp.float32)
    owner = jax.random.randint(seeds[1], (STEPS,), 0, N_BAND).astype(jnp.int32)
    picks = touch_ends(jax.random.randint(seeds[2], (STEPS, 2), 0, BLOC), jax.random.fold_in(seeds[2], 1), 0, BLOC - 1).astype(jnp.int32)
    return dict(orbitals=orbitals, owner=owner, picks=picks)


length_first = 41.05
length_side = 41.05
length_last = 20.525
omega_screen = 0.106


def frequency(counter, length):
    return jnp.where(counter <= length // 2, counter, counter - length).astype(jnp.float32)


def coulomb_kernel(freq_z, freq_y, freq_x):
    wave_first = 2.0 * math.pi / length_first
    wave_side = 2.0 * math.pi / length_side
    wave_last = 2.0 * math.pi / length_last
    squared = (wave_first * freq_z)[:, None, None] ** 2 + (wave_side * freq_y)[None, :, None] ** 2 + (wave_last * freq_x)[None, None, :] ** 2
    safe = jnp.where(squared > 0, squared, 1.0)
    screened = -4.0 * math.pi * jnp.expm1(-squared / (4.0 * omega_screen ** 2)) / safe
    return jnp.where(squared > 0, screened, math.pi / omega_screen ** 2)


def reference(orbitals, owner, picks):
    kernel = coulomb_kernel(frequency(jnp.arange(NZ), NZ), frequency(jnp.arange(NY), NY), frequency(jnp.arange(NX), NX))
    exchange_sum = jnp.zeros_like(orbitals)
    collected = []
    for turn_index in range(STEPS):
        chosen_rows = (owner[turn_index] * BLOC + picks[turn_index]).astype(jnp.int32)
        chosen = jnp.take(orbitals, chosen_rows, axis=0)

        def accumulate(running, orbital):
            density = lax.complex(orbital * chosen[0], orbital * chosen[1]).reshape(NZ, NY, NX)
            potential = jnp.fft.ifftn(kernel * jnp.fft.fftn(density)).reshape(NZ, NY * NX)
            first_part = jnp.real(potential)
            second_part = jnp.imag(potential)
            running = running + jnp.stack([first_part * orbital, second_part * orbital])
            return running, first_part * chosen[0] + second_part * chosen[1]

        start_sum = jnp.zeros((2, NZ, NY * NX), orbitals.dtype)
        summed, applied = lax.scan(accumulate, start_sum, orbitals)
        exchange_sum = exchange_sum + applied
        collected.append(summed)
    return exchange_sum, jnp.stack(collected)
```

```python
import math

import jax
import jax.numpy as jnp
from jax import lax
from jax.sharding import Mesh, PartitionSpec as P

NX = 48
NY = 96
NZ = 96
STEPS = 2


length_first = 41.05
length_side = 41.05
length_last = 20.525
omega_screen = 0.106


def swap(x, axis, bit):
    size = lax.axis_size(axis)
    return lax.ppermute(x, axis, [(i, i ^ bit) for i in range(size)])


def split_sum(x, axis, bit):
    upper = (lax.axis_index(axis) & bit) != 0
    middle = x.shape[-1] // 2
    first, second = x[..., :middle], x[..., middle:]
    kept = jnp.where(upper, second, first)
    other = jnp.where(upper, first, second)
    return kept + swap(other, axis, bit)


def join(x, axis, bit):
    upper = (lax.axis_index(axis) & bit) != 0
    other = swap(x, axis, bit)
    return jnp.concatenate([jnp.where(upper, other, x), jnp.where(upper, x, other)], axis=-1)


def sum_over_bands(x):
    core = lax.axis_index("c")
    kept = jnp.where(core == 0, x[0], x[1])
    other = jnp.where(core == 0, x[1], x[0])
    part = kept + swap(other, "c", 1)
    part = split_sum(part, "z", 1)
    part = split_sum(part, "xl", 1)
    part = part + swap(part, "z", 2)
    part = part + swap(part, "z", 4)
    part = join(part, "xl", 1)
    part = join(part, "z", 1)
    other = swap(part, "c", 1)
    return jnp.stack([jnp.where(core == 0, part, other), jnp.where(core == 0, other, part)])


def frequency(counter, length):
    return jnp.where(counter <= length // 2, counter, counter - length).astype(jnp.float32)


def coulomb_kernel(freq_z, freq_y, freq_x):
    wave_first = 2.0 * math.pi / length_first
    wave_side = 2.0 * math.pi / length_side
    wave_last = 2.0 * math.pi / length_last
    squared = (
        (wave_first * freq_z)[:, None, None] ** 2
        + (wave_side * freq_y)[None, :, None] ** 2
        + (wave_last * freq_x)[None, None, :] ** 2
    )
    safe = jnp.where(squared > 0, squared, 1.0)
    screened = -4.0 * math.pi * jnp.expm1(-squared / (4.0 * omega_screen**2)) / safe
    return jnp.where(squared > 0, screened, math.pi / omega_screen**2)


def dft_table(length, direction):
    counter = jnp.arange(length)
    product = counter[:, None] * counter[None, :] % length
    angle = 2.0 * math.pi / length * product.astype(jnp.float32)
    return (jnp.cos(angle), direction * jnp.sin(angle))


def along_last(values, length, direction):
    cosines, sine_table = dft_table(length, direction)
    upper = jnp.concatenate([cosines, -sine_table], axis=1)
    lower = jnp.concatenate([sine_table, cosines], axis=1)
    matrix = jnp.concatenate([upper, lower], axis=0)
    return jnp.matmul(values, matrix, precision=lax.Precision.HIGHEST)


def along_axis(values, length, direction, pattern):
    cosines, sine_table = dft_table(length, direction)
    middle = values.shape[-1] // 2
    with_cos = jnp.einsum(pattern, cosines, values, precision=lax.Precision.HIGHEST)
    with_sin = jnp.einsum(pattern, sine_table, values, precision=lax.Precision.HIGHEST)
    real_part = with_cos[..., :middle] + with_sin[..., middle:]
    imag_part = with_cos[..., middle:] - with_sin[..., :middle]
    return jnp.concatenate([real_part, imag_part], axis=-1)


def per_device(orbitals, owner, picks):
    bloc, planes, points = orbitals.shape
    slab_count = 8
    column_rows = NY // slab_count
    slab_index = lax.axis_index("xh") * 4 + lax.axis_index("y")
    freq_y = frequency(slab_index * column_rows + jnp.arange(column_rows), NY)
    kernel = coulomb_kernel(frequency(jnp.arange(NZ), NZ), freq_y, frequency(jnp.arange(NX), NX))
    kernel = kernel * (1.0 / (NX * NY * NZ))
    kernel_tile = jnp.concatenate([kernel, kernel], axis=-1)
    exchange_sum = jnp.zeros_like(orbitals)
    collected = []
    group = (lax.axis_index("z") * 2 + lax.axis_index("xl")) * 2 + lax.axis_index("c")
    picked = jnp.take(orbitals, picks.reshape(-1), axis=0).reshape(STEPS, 2, planes, points)
    mine = (owner == group)[:, None, None, None]
    picked = jnp.where(mine, picked, 0.0).reshape(STEPS, 2 * planes, points)
    chosen_all = sum_over_bands(picked).reshape(STEPS, 2, planes, points)
    for turn_index in range(STEPS):
        chosen = chosen_all[turn_index]
        real_part = (orbitals * chosen[0]).reshape(bloc, planes, NY, NX)
        imag_part = (orbitals * chosen[1]).reshape(bloc, planes, NY, NX)
        fields = jnp.concatenate([real_part, imag_part], axis=-1)
        fields = along_last(fields, NX, 1.0)
        fields = along_axis(fields, NY, 1.0, "ky,bzyx->bzkx")
        columns = lax.all_to_all(fields, ("xh", "y"), split_axis=2, concat_axis=1, tiled=True)
        columns = along_axis(columns, NZ, 1.0, "kz,bzyx->bkyx") * kernel_tile
        columns = along_axis(columns, NZ, -1.0, "kz,bzyx->bkyx")
        fields = lax.all_to_all(columns, ("xh", "y"), split_axis=1, concat_axis=2, tiled=True)
        fields = along_axis(fields, NY, -1.0, "ky,bzyx->bzkx")
        fields = along_last(fields, NX, -1.0)
        count = fields.shape[0]
        potentials_first_part = fields[..., :NX].reshape(count, planes, points)
        potentials_second_part = fields[..., NX:].reshape(count, planes, points)
        applied = potentials_first_part * chosen[0] + potentials_second_part * chosen[1]
        contributions_local_sum = jnp.stack(
            [
                jnp.sum(potentials_first_part * orbitals, axis=0),
                jnp.sum(potentials_second_part * orbitals, axis=0),
            ]
        )
        applied, local_sum = (applied, contributions_local_sum)
        exchange_sum = exchange_sum + applied
        collected.append(local_sum.reshape(2 * planes, points))
    transposed = sum_over_bands(jnp.stack(collected)).reshape(STEPS, 2, planes, points)
    return (exchange_sum, transposed)


def solution(mesh):
    fine = Mesh(mesh.devices.reshape(8, 2, 2, 2, 4), ("z", "xl", "c", "xh", "y"))
    band, slab = ("z", "xl", "c"), ("xh", "y")
    in_specs = (P(band, slab, None), P(), P())
    out_specs = (P(band, slab, None), P(None, None, slab, None))
    return jax.shard_map(
        per_device, mesh=fine, in_specs=in_specs, out_specs=out_specs, check_vma=False
    )
```

```python
import functools
import math

import jax
import jax.numpy as jnp
import ml_dtypes
import numpy as np
from jax import lax
from jax.experimental import pallas as pl
from jax.experimental.pallas import tpu as pltpu
from jax.sharding import Mesh, PartitionSpec as P

NX = 48
NY = 96
NZ = 96
BLOC = 4
STEPS = 2
SLABS = 8
PLANES = NZ // SLABS
POINTS = NY * NX
ROWS = BLOC * PLANES
PAIR = 2 * PLANES
BLOCKS = 12
INNER = 8
LANES = INNER * NX
HALF = LANES // 2
COLUMNS = 3 * LANES

length_first = 41.05
length_side = 41.05
length_last = 20.525
omega_screen = 0.106


def swap(x, axis, bit):
    size = lax.axis_size(axis)
    return lax.ppermute(x, axis, [(i, i ^ bit) for i in range(size)])


def split_sum(x, axis, bit):
    upper = (lax.axis_index(axis) & bit) != 0
    middle = x.shape[-1] // 2
    first, second = x[..., :middle], x[..., middle:]
    kept = jnp.where(upper, second, first)
    other = jnp.where(upper, first, second)
    return kept + swap(other, axis, bit)


def join(x, axis, bit):
    upper = (lax.axis_index(axis) & bit) != 0
    other = swap(x, axis, bit)
    return jnp.concatenate([jnp.where(upper, other, x), jnp.where(upper, x, other)], axis=-1)


def sum_over_bands(x):
    core = lax.axis_index("c")
    kept = jnp.where(core == 0, x[0], x[1])
    other = jnp.where(core == 0, x[1], x[0])
    part = kept + swap(other, "c", 1)
    part = split_sum(part, "z", 1)
    part = split_sum(part, "xl", 1)
    part = part + swap(part, "z", 2)
    part = part + swap(part, "z", 4)
    part = join(part, "xl", 1)
    part = join(part, "z", 1)
    other = swap(part, "c", 1)
    return jnp.stack([jnp.where(core == 0, part, other), jnp.where(core == 0, other, part)])


def frequency(counter, length):
    return jnp.where(counter <= length // 2, counter, counter - length).astype(jnp.float32)


def coulomb_kernel(freq_z, freq_y, freq_x):
    squared = (
        (2.0 * math.pi / length_first * freq_z) ** 2
        + (2.0 * math.pi / length_side * freq_y) ** 2
        + (2.0 * math.pi / length_last * freq_x) ** 2
    )
    safe = jnp.where(squared > 0, squared, 1.0)
    screened = -4.0 * math.pi * jnp.expm1(-squared / (4.0 * omega_screen**2)) / safe
    return jnp.where(squared > 0, screened, math.pi / omega_screen**2)


def kernel_columns(xh, y):
    kz = (jnp.arange(SLABS)[:, None] * PLANES + jnp.arange(PLANES)[None, :]).reshape(NZ, 1)
    lane = jnp.arange(3 * HALF)
    kb = 3 * y + lane // HALF
    kk = 4 * xh + lane % HALF // NX
    values = coulomb_kernel(
        frequency(kz, NZ), frequency(kb + BLOCKS * kk, NY)[None, :], frequency(lane % NX, NX)[None, :]
    ) * (1.0 / (NX * NY * NZ))
    values = values.reshape(SLABS, 1, PLANES, 3, 1, HALF)
    return jnp.broadcast_to(values, (SLABS, 2, PLANES, 3, 2, HALF)).reshape(2 * NZ, COLUMNS)


def split_table(table):
    high = table.astype(ml_dtypes.bfloat16)
    low = (table - high.astype(np.float64)).astype(ml_dtypes.bfloat16)
    return high, low


@functools.cache
def tables():
    inner, x = np.divmod(np.arange(LANES), NX)
    angle = -2.0 * np.pi * (
        (inner[:, None] * inner[None, :] % INNER) / INNER + (x[:, None] * x[None, :] % NX) / NX
    )
    real, imag = np.cos(angle), np.sin(angle)
    forward = np.zeros((2, LANES, 2, 2, HALF))
    inverse = np.zeros((2, 2, HALF, 2, LANES))
    for half in range(2):
        part = slice(half * HALF, (half + 1) * HALF)
        forward[0, :, half, 0], forward[1, :, half, 0] = real[:, part], -imag[:, part]
        forward[0, :, half, 1], forward[1, :, half, 1] = imag[:, part], real[:, part]
        inverse[half, 0, :, 0], inverse[half, 1, :, 0] = real[part], imag[part]
        inverse[half, 0, :, 1], inverse[half, 1, :, 1] = -imag[part], real[part]
    forward = split_table(forward.reshape(2 * LANES, 2 * LANES))
    inverse = split_table(inverse.reshape(2 * LANES, 2 * LANES))
    turn = -2.0 * np.pi / NY * (np.arange(BLOCKS)[:, None] * inner[None, :] % NY)
    twiddle = np.cos(turn).astype(np.float32), np.sin(turn).astype(np.float32)
    slab, rest = np.divmod(np.arange(2 * NZ), PAIR)
    band, plane = np.divmod(rest, PLANES)
    z = slab * PLANES + plane
    same = band[:, None] == band[None, :]
    angle = 2.0 * np.pi / NZ * (z[:, None] * z[None, :] % NZ)
    stacked = np.concatenate([np.where(same, np.cos(angle), 0), np.where(same, np.sin(angle), 0)])
    high, low = split_table(stacked)
    along_z = np.concatenate([high, high, low], axis=1)
    return forward, inverse, twiddle, along_z


def split(x):
    high = x.astype(jnp.bfloat16)
    return high, (x - high.astype(jnp.float32)).astype(jnp.bfloat16)


def dot(a, b):
    return lax.dot_general(a, b, (((1,), (0,)), ((), ())), preferred_element_type=jnp.float32)


def dft12(values, sign):
    def turn(value):
        re, im = value
        return (-im, re) if sign > 0 else (im, -re)

    def add(a, b):
        return a[0] + b[0], a[1] + b[1]

    def sub(a, b):
        return a[0] - b[0], a[1] - b[1]

    quarter = []
    for n1 in range(3):
        a = [values[(4 * n1 + 3 * n2) % 12] for n2 in range(4)]
        even, odd = add(a[0], a[2]), add(a[1], a[3])
        left, right = sub(a[0], a[2]), turn(sub(a[1], a[3]))
        quarter.append([add(even, odd), add(left, right), sub(even, odd), sub(left, right)])
    result = [None] * 12
    for k4 in range(4):
        b = [quarter[n1][k4] for n1 in range(3)]
        total = add(b[1], b[2])
        difference = sub(b[1], b[2])
        middle = (b[0][0] - 0.5 * total[0], b[0][1] - 0.5 * total[1])
        scale = math.sqrt(0.75)
        side = turn((scale * difference[0], scale * difference[1]))
        for k3, value in enumerate((add(b[0], total), add(middle, side), sub(middle, side))):
            where = next(k for k in range(12) if k % 3 == k3 and k % 4 == k4)
            result[where] = value
    return result


def forward_kernel(orbital_ref, chosen_ref, cos_ref, sin_ref, high_ref, low_ref, out_ref, field, field_high, field_low):
    steps = chosen_ref.shape[0]
    for step in range(steps):

        def tile(index, carry):
            for group in range(2):
                for part in range(3):
                    rows = pl.ds(pl.multiple_of(group * PAIR + index * 8, 8), 8)
                    own = pl.ds(pl.multiple_of(index * 8, 8), 8)
                    values = []
                    for block in range(BLOCKS):
                        lanes = pl.ds(block * LANES + part * 128, 128)
                        orbital = orbital_ref[rows, lanes]
                        values.append(
                            (orbital * chosen_ref[step, 0, own, lanes], orbital * chosen_ref[step, 1, own, lanes])
                        )
                    values = dft12(values, -1)
                    for kb, (re, im) in enumerate(values):
                        cosine = cos_ref[kb : kb + 1, part * 128 : part * 128 + 128]
                        sine = sin_ref[kb : kb + 1, part * 128 : part * 128 + 128]
                        to = pl.ds(pl.multiple_of(kb * ROWS + group * PAIR + index * 8, 8), 8)
                        field[to, pl.ds(part * 128, 128)] = re * cosine - im * sine
                        field[to, pl.ds(LANES + part * 128, 128)] = re * sine + im * cosine
            return carry

        lax.fori_loop(0, PAIR // 8, tile, 0)
        field_high[...], field_low[...] = split(field[...])
        for piece in range(3):
            lanes = pl.ds(piece * 256, 256)
            high = high_ref[:, lanes]
            result = dot(field_high[...], high) + dot(field_low[...], high) + dot(field_high[...], low_ref[:, lanes])
            for part in range(2):
                half, offset = divmod(2 * piece + part, 3)
                for kb in range(BLOCKS):
                    column, turn = divmod(kb, 3)
                    out_ref[
                        half * 4 + column, pl.ds(step * ROWS, ROWS), pl.ds(turn * LANES + offset * 128, 128)
                    ] = result[kb * ROWS : kb * ROWS + ROWS, part * 128 : part * 128 + 128]


def middle_kernel(value_ref, kernel_ref, table_ref, out_ref):
    rows = value_ref.shape[1]
    imaginary = lax.broadcasted_iota(jnp.int32, (2 * NZ, LANES), 1) >= HALF

    def swapped(x):
        return jnp.concatenate([x[:, HALF:], x[:, :HALF]], axis=1)

    def transform(x, sign):
        high, low = split(x)
        both = dot(table_ref[...], jnp.concatenate([high, low, high], axis=0))
        cosine, sine = both[: 2 * NZ], swapped(both[2 * NZ :])
        return cosine + jnp.where(imaginary, -sign * sine, sign * sine)

    for group in range(rows // PAIR):
        own = slice(group * PAIR, group * PAIR + PAIR)
        for turn in range(3):
            lanes = slice(turn * LANES, turn * LANES + LANES)
            x = jnp.concatenate([value_ref[slab, own, lanes] for slab in range(SLABS)], axis=0)
            x = transform(x, 1.0) * kernel_ref[:, lanes]
            x = transform(x, -1.0)
            for slab in range(SLABS):
                out_ref[slab, own, lanes] = x[slab * PAIR : slab * PAIR + PAIR]


def inverse_kernel(
    value_ref, orbital_ref, chosen_ref, cos_ref, sin_ref, high_ref, low_ref, applied_ref, summed_ref, field_high, field_low, field, totals
):
    steps = chosen_ref.shape[0]
    for step in range(steps):
        for kb in range(BLOCKS):
            column, turn = divmod(kb, 3)
            for half in range(2):
                x = value_ref[half * 4 + column, pl.ds(step * ROWS, ROWS), pl.ds(turn * LANES, LANES)]
                high, low = split(x)
                field_high[kb * ROWS : kb * ROWS + ROWS, half * LANES : half * LANES + LANES] = high
                field_low[kb * ROWS : kb * ROWS + ROWS, half * LANES : half * LANES + LANES] = low
        for piece in range(3):
            lanes = pl.ds(piece * 256, 256)
            high = high_ref[:, lanes]
            field[:, lanes] = (
                dot(field_high[...], high) + dot(field_low[...], high) + dot(field_high[...], low_ref[:, lanes])
            )

        def tile(index, carry):
            own = pl.ds(pl.multiple_of(index * 8, 8), 8)
            for part in range(3):
                for group in range(2):
                    rows = pl.ds(pl.multiple_of(group * PAIR + index * 8, 8), 8)
                    values = []
                    for kb in range(BLOCKS):
                        cosine = cos_ref[kb : kb + 1, part * 128 : part * 128 + 128]
                        sine = sin_ref[kb : kb + 1, part * 128 : part * 128 + 128]
                        at = pl.ds(pl.multiple_of(kb * ROWS + group * PAIR + index * 8, 8), 8)
                        re = field[at, pl.ds(part * 128, 128)]
                        im = field[at, pl.ds(LANES + part * 128, 128)]
                        values.append((re * cosine + im * sine, im * cosine - re * sine))
                    values = dft12(values, 1)
                    for block, (first, second) in enumerate(values):
                        lanes = pl.ds(block * LANES + part * 128, 128)
                        orbital = orbital_ref[rows, lanes]
                        applied = first * chosen_ref[step, 0, own, lanes] + second * chosen_ref[step, 1, own, lanes]
                        if step == 0:
                            applied_ref[rows, lanes] = applied
                        else:
                            applied_ref[rows, lanes] += applied
                        if group == 0:
                            totals[0, own, lanes] = first * orbital
                            totals[1, own, lanes] = second * orbital
                        else:
                            totals[0, own, lanes] += first * orbital
                            totals[1, own, lanes] += second * orbital
            return carry

        lax.fori_loop(0, PAIR // 8, tile, 0)
        for block in range(BLOCKS):
            lanes = pl.ds(block * LANES, LANES)
            first = totals[0, :PLANES, lanes] + totals[0, PLANES:, lanes]
            second = totals[1, :PLANES, lanes] + totals[1, PLANES:, lanes]
            summed_ref[step, :, lanes] = jnp.concatenate([first, second], axis=0)


PARAMS = dict(compiler_params=pltpu.CompilerParams(vmem_limit_bytes=48 * 1024 * 1024))
VMEM = pl.BlockSpec(memory_space=pltpu.VMEM)


def cost(operations, size):
    return pl.CostEstimate(flops=operations, bytes_accessed=size, transcendentals=0)


def to_columns(orbitals, chosen):
    steps = chosen.shape[0]
    forward, _, twiddle, _ = tables()
    tall = BLOCKS * ROWS
    return pl.pallas_call(
        forward_kernel,
        out_shape=jax.ShapeDtypeStruct((SLABS, steps * ROWS, COLUMNS), jnp.float32),
        in_specs=[VMEM] * 6,
        out_specs=VMEM,
        scratch_shapes=[
            pltpu.VMEM((tall, 2 * LANES), jnp.float32),
            pltpu.VMEM((tall, 2 * LANES), jnp.bfloat16),
            pltpu.VMEM((tall, 2 * LANES), jnp.bfloat16),
        ],
        cost_estimate=cost(steps * 6 * tall * (2 * LANES) ** 2, steps * 4_000_000),
        **PARAMS,
    )(orbitals, chosen, *twiddle, *forward)


def screened(values, kernel):
    _, _, _, along_z = tables()
    return pl.pallas_call(
        middle_kernel,
        out_shape=jax.ShapeDtypeStruct(values.shape, jnp.float32),
        in_specs=[VMEM] * 3,
        out_specs=VMEM,
        cost_estimate=cost(values.shape[1] // PAIR * 4 * 4 * NZ * 6 * NZ * COLUMNS, 8 * values.size),
        **PARAMS,
    )(values, kernel, along_z)


def from_columns(values, orbitals, chosen):
    steps = chosen.shape[0]
    _, inverse, twiddle, _ = tables()
    tall = BLOCKS * ROWS
    return pl.pallas_call(
        inverse_kernel,
        out_shape=(
            jax.ShapeDtypeStruct((ROWS, POINTS), jnp.float32),
            jax.ShapeDtypeStruct((steps, PAIR, POINTS), jnp.float32),
        ),
        in_specs=[VMEM] * 7,
        out_specs=(VMEM, VMEM),
        scratch_shapes=[
            pltpu.VMEM((tall, 2 * LANES), jnp.bfloat16),
            pltpu.VMEM((tall, 2 * LANES), jnp.bfloat16),
            pltpu.VMEM((tall, 2 * LANES), jnp.float32),
            pltpu.VMEM((2, PAIR, POINTS), jnp.float32),
        ],
        cost_estimate=cost(steps * 6 * tall * (2 * LANES) ** 2, steps * 4_000_000),
        **PARAMS,
    )(values, orbitals, chosen, *twiddle, *inverse)


def per_device(orbitals, owner, picks):
    group = (lax.axis_index("z") * 2 + lax.axis_index("xl")) * 2 + lax.axis_index("c")
    picked = jnp.take(orbitals, picks.reshape(-1), axis=0).reshape(STEPS, 2, PLANES, POINTS)
    mine = (owner == group)[:, None, None, None]
    picked = jnp.where(mine, picked, 0.0).reshape(STEPS, PAIR, POINTS)
    chosen = sum_over_bands(picked).reshape(STEPS, 2, PLANES, POINTS)
    chosen = jnp.concatenate([chosen, chosen], axis=2)
    kernel = kernel_columns(lax.axis_index("xh"), lax.axis_index("y"))
    flat = orbitals.reshape(ROWS, POINTS)
    columns = to_columns(flat, chosen)
    columns = lax.all_to_all(columns, ("xh", "y"), split_axis=0, concat_axis=0, tiled=True)
    columns = screened(columns, kernel)
    columns = lax.all_to_all(columns, ("xh", "y"), split_axis=0, concat_axis=0, tiled=True)
    applied, local_sum = from_columns(columns, flat, chosen)
    transposed = sum_over_bands(local_sum).reshape(STEPS, 2, PLANES, POINTS)
    return applied.reshape(BLOC, PLANES, POINTS), transposed


def solution(mesh):
    fine = Mesh(mesh.devices.reshape(8, 2, 2, 2, 4), ("z", "xl", "c", "xh", "y"))
    band, slab = ("z", "xl", "c"), ("xh", "y")
    in_specs = (P(band, slab, None), P(), P())
    out_specs = (P(band, slab, None), P(None, None, slab, None))
    return jax.shard_map(
        per_device, mesh=fine, in_specs=in_specs, out_specs=out_specs, check_vma=False
    )
```

```python
import functools
import math

import jax
import jax.numpy as jnp
import ml_dtypes
import numpy as np
from jax import lax
from jax.experimental import pallas as pl
from jax.experimental.pallas import tpu as pltpu
from jax.sharding import Mesh, PartitionSpec as P

NX = 48
NY = 96
NZ = 96
BLOC = 4
STEPS = 2
SLABS = 8
PLANES = NZ // SLABS
POINTS = NY * NX
ROWS = BLOC * PLANES
PAIR = 2 * PLANES
BLOCKS = 12
INNER = 8
LANES = INNER * NX
HALF = LANES // 2
COLUMNS = 3 * LANES
MIDDLE = POINTS // 2

length_first = 41.05
length_side = 41.05
length_last = 20.525
omega_screen = 0.106


def swap(x, axis, bit):
    size = lax.axis_size(axis)
    return lax.ppermute(x, axis, [(i, i ^ bit) for i in range(size)])


def near(x, bits):
    z_count, x_count = lax.axis_size("z"), lax.axis_size("xl")
    pairs = [
        (z * x_count + x, (z ^ (bits >> 1)) * x_count + (x ^ (bits & 1)))
        for z in range(z_count)
        for x in range(x_count)
    ]
    return lax.ppermute(x, ("z", "xl"), pairs)


def along(x, distance):
    size = lax.axis_size("z")
    return lax.ppermute(x, "z", [(i, (i + distance) % size) for i in range(size)])


def pick(pieces, index):
    low = jnp.where(index == 0, pieces[0], pieces[1])
    high = jnp.where(index == 2, pieces[2], pieces[3])
    return jnp.where(index < 2, low, high)


def tie(*values):
    return lax.optimization_barrier(values)


def join_cores(kept, sent):
    return kept + swap(sent, "c", 1)


def join_near(half):
    spot = lax.axis_index("z") % 2 * 2 + lax.axis_index("xl")
    width = half.shape[1] // 4
    quarters = [half[:, i * width : (i + 1) * width] for i in range(4)]
    arrived = [near(pick(quarters, spot ^ bits), bits) for bits in (1, 2, 3)]
    return pick(quarters, spot) + arrived[0] + arrived[1] + arrived[2]


def join_far(part):
    arrived = [along(part, distance) for distance in (2, 4, 6)]
    return part + arrived[0] + arrived[1] + arrived[2]


def spread_near(part):
    spot = lax.axis_index("z") % 2 * 2 + lax.axis_index("xl")
    quarters = [part] + [near(part, bits) for bits in (1, 2, 3)]
    return jnp.concatenate([pick(quarters, spot ^ i) for i in range(4)], axis=1)


def frequency(counter, length):
    return jnp.where(counter <= length // 2, counter, counter - length).astype(jnp.float32)


def coulomb_kernel(freq_z, freq_y, freq_x):
    squared = (
        (2.0 * math.pi / length_first * freq_z) ** 2
        + (2.0 * math.pi / length_side * freq_y) ** 2
        + (2.0 * math.pi / length_last * freq_x) ** 2
    )
    safe = jnp.where(squared > 0, squared, 1.0)
    screened = -4.0 * math.pi * jnp.expm1(-squared / (4.0 * omega_screen**2)) / safe
    return jnp.where(squared > 0, screened, math.pi / omega_screen**2)


def kernel_columns(xh, y):
    row = jnp.arange(2 * NZ)[:, None]
    lane = jnp.arange(COLUMNS)[None, :]
    kz = row // PAIR * PLANES + row % PLANES
    kb = 3 * y + lane // LANES
    kk = 4 * xh + lane % HALF // NX
    return coulomb_kernel(
        frequency(kz, NZ), frequency(kb + BLOCKS * kk, NY), frequency(lane % NX, NX)
    ) * (1.0 / (NX * NY * NZ))


def split_table(table):
    high = table.astype(ml_dtypes.bfloat16)
    low = (table - high.astype(np.float64)).astype(ml_dtypes.bfloat16)
    return high, low


@functools.cache
def tables():
    inner, x = np.divmod(np.arange(LANES), NX)
    angle = -2.0 * np.pi * (
        (inner[:, None] * inner[None, :] % INNER) / INNER + (x[:, None] * x[None, :] % NX) / NX
    )
    real, imag = np.cos(angle), np.sin(angle)
    forward = np.zeros((2, LANES, 2, 2, HALF))
    inverse = np.zeros((2, 2, HALF, 2, LANES))
    for half in range(2):
        part = slice(half * HALF, (half + 1) * HALF)
        forward[0, :, half, 0], forward[1, :, half, 0] = real[:, part], -imag[:, part]
        forward[0, :, half, 1], forward[1, :, half, 1] = imag[:, part], real[:, part]
        inverse[half, 0, :, 0], inverse[half, 1, :, 0] = real[part], imag[part]
        inverse[half, 0, :, 1], inverse[half, 1, :, 1] = -imag[part], real[part]
    forward = split_table(forward.reshape(2 * LANES, 2 * LANES))
    inverse = split_table(inverse.reshape(2 * LANES, 2 * LANES))
    turn = -2.0 * np.pi / NY * (np.arange(BLOCKS)[:, None] * inner[None, :] % NY)
    twiddle = np.cos(turn).astype(np.float32), np.sin(turn).astype(np.float32)
    slab, rest = np.divmod(np.arange(2 * NZ), PAIR)
    band, plane = np.divmod(rest, PLANES)
    z = slab * PLANES + plane
    same = band[:, None] == band[None, :]
    angle = 2.0 * np.pi / NZ * (z[:, None] * z[None, :] % NZ)
    stacked = np.concatenate([np.where(same, np.cos(angle), 0), np.where(same, np.sin(angle), 0)])
    high, low = split_table(stacked)
    along_z = np.concatenate([high, high, low], axis=1)
    return forward, inverse, twiddle, along_z


def split(x):
    high = x.astype(jnp.bfloat16)
    return high, (x - high.astype(jnp.float32)).astype(jnp.bfloat16)


def dot(a, b):
    return lax.dot_general(a, b, (((1,), (0,)), ((), ())), preferred_element_type=jnp.float32)


def dft12(values, sign):
    def turn(value):
        re, im = value
        return (-im, re) if sign > 0 else (im, -re)

    def add(a, b):
        return a[0] + b[0], a[1] + b[1]

    def sub(a, b):
        return a[0] - b[0], a[1] - b[1]

    quarter = []
    for n1 in range(3):
        a = [values[(4 * n1 + 3 * n2) % 12] for n2 in range(4)]
        even, odd = add(a[0], a[2]), add(a[1], a[3])
        left, right = sub(a[0], a[2]), turn(sub(a[1], a[3]))
        quarter.append([add(even, odd), add(left, right), sub(even, odd), sub(left, right)])
    result = [None] * 12
    for k4 in range(4):
        b = [quarter[n1][k4] for n1 in range(3)]
        total = add(b[1], b[2])
        difference = sub(b[1], b[2])
        middle = (b[0][0] - 0.5 * total[0], b[0][1] - 0.5 * total[1])
        scale = math.sqrt(0.75)
        side = turn((scale * difference[0], scale * difference[1]))
        for k3, value in enumerate((add(b[0], total), add(middle, side), sub(middle, side))):
            where = next(k for k in range(12) if k % 3 == k3 and k % 4 == k4)
            result[where] = value
    return result


def forward_kernel(
    here_ref, orbital_ref, half_ref, other_ref, cos_ref, sin_ref, high_source, low_source,
    out_ref, chosen_ref, field, field_high, field_low, high_ref, low_ref, loaded,
):
    loads = [
        pltpu.make_async_copy(source, target, loaded.at[index])
        for index, (source, target) in enumerate(((high_source, high_ref), (low_source, low_ref)))
    ]
    for load in loads:
        load.start()
    core = here_ref[1]
    for step in range(STEPS):
        for offset in range(0, MIDDLE, LANES):
            for where, source in ((core, half_ref), (1 - core, other_ref)):
                lanes = pl.ds(pl.multiple_of(where * MIDDLE + offset, 128), LANES)
                for a in range(2):
                    first = (step * 2 + a) * PLANES
                    rows = source[first : first + PLANES, offset : offset + LANES]
                    chosen_ref[step, a, :, lanes] = jnp.concatenate([rows, rows], axis=0)

    for step in range(STEPS):

        def tile(index, carry):
            for group in range(2):
                for part in range(3):
                    rows = pl.ds(pl.multiple_of(group * PAIR + index * 8, 8), 8)
                    own = pl.ds(pl.multiple_of(index * 8, 8), 8)
                    values = []
                    for block in range(BLOCKS):
                        lanes = pl.ds(block * LANES + part * 128, 128)
                        orbital = orbital_ref[rows, lanes]
                        values.append(
                            (orbital * chosen_ref[step, 0, own, lanes], orbital * chosen_ref[step, 1, own, lanes])
                        )
                    values = dft12(values, -1)
                    for kb, (re, im) in enumerate(values):
                        cosine = cos_ref[kb : kb + 1, part * 128 : part * 128 + 128]
                        sine = sin_ref[kb : kb + 1, part * 128 : part * 128 + 128]
                        to = pl.ds(pl.multiple_of(kb * ROWS + group * PAIR + index * 8, 8), 8)
                        field[to, pl.ds(part * 128, 128)] = re * cosine - im * sine
                        field[to, pl.ds(LANES + part * 128, 128)] = re * sine + im * cosine
            return carry

        lax.fori_loop(0, PAIR // 8, tile, 0)
        field_high[...], field_low[...] = split(field[...])
        if step == 0:
            for load in loads:
                load.wait()
        for piece in range(3):
            lanes = pl.ds(piece * 256, 256)
            high = high_ref[:, lanes]
            result = dot(field_high[...], high) + dot(field_low[...], high) + dot(field_high[...], low_ref[:, lanes])
            for part in range(2):
                half, offset = divmod(2 * piece + part, 3)
                for kb in range(BLOCKS):
                    column, turn = divmod(kb, 3)
                    out_ref[
                        half * 4 + column, pl.ds(step * ROWS, ROWS), pl.ds(turn * LANES + offset * 128, 128)
                    ] = result[kb * ROWS : kb * ROWS + ROWS, part * 128 : part * 128 + 128]


def middle_kernel(step, value_ref, kernel_ref, table_ref, out_ref):
    imaginary = lax.broadcasted_iota(jnp.int32, (2 * NZ, LANES), 1) >= HALF

    def swapped(x):
        return jnp.concatenate([x[:, HALF:], x[:, :HALF]], axis=1)

    def transform(x, sign):
        high, low = split(x)
        both = dot(table_ref[...], jnp.concatenate([high, low, high], axis=0))
        cosine, sine = both[: 2 * NZ], swapped(both[2 * NZ :])
        return cosine + jnp.where(imaginary, -sign * sine, sign * sine)

    for group in range(ROWS // PAIR):
        source = slice(step * ROWS + group * PAIR, step * ROWS + group * PAIR + PAIR)
        own = slice(group * PAIR, group * PAIR + PAIR)
        for turn in range(3):
            lanes = slice(turn * LANES, turn * LANES + LANES)
            x = jnp.concatenate([value_ref[slab, source, lanes] for slab in range(SLABS)], axis=0)
            x = transform(x, 1.0) * kernel_ref[:, lanes]
            x = transform(x, -1.0)
            for slab in range(SLABS):
                out_ref[slab, own, lanes] = x[slab * PAIR : slab * PAIR + PAIR]


def inverse_kernel(
    step, here_ref, value_ref, orbital_ref, chosen_ref, cos_ref, sin_ref, high_source, low_source, *rest
):
    if step == 0:
        applied_ref, kept_ref, sent_ref, field_high, field_low, field, totals, high_ref, low_ref, loaded = rest
        sums = applied_ref
    else:
        before_ref, applied_ref, kept_ref, sent_ref, field_high, field_low, field, totals, high_ref, low_ref, loaded, sums = rest
    loads = [
        pltpu.make_async_copy(source, target, loaded.at[index])
        for index, (source, target) in enumerate(((high_source, high_ref), (low_source, low_ref)))
    ]
    for load in loads:
        load.start()
    for kb in range(BLOCKS):
        column, turn = divmod(kb, 3)
        for half in range(2):
            x = value_ref[half * 4 + column, :, pl.ds(turn * LANES, LANES)]
            high, low = split(x)
            field_high[kb * ROWS : kb * ROWS + ROWS, half * LANES : half * LANES + LANES] = high
            field_low[kb * ROWS : kb * ROWS + ROWS, half * LANES : half * LANES + LANES] = low
    for load in loads:
        load.wait()
    for piece in range(3):
        lanes = pl.ds(piece * 256, 256)
        high = high_ref[:, lanes]
        field[:, lanes] = (
            dot(field_high[...], high) + dot(field_low[...], high) + dot(field_high[...], low_ref[:, lanes])
        )

    def tile(index, carry):
        own = pl.ds(pl.multiple_of(index * 8, 8), 8)
        for part in range(3):
            for group in range(2):
                rows = pl.ds(pl.multiple_of(group * PAIR + index * 8, 8), 8)
                values = []
                for kb in range(BLOCKS):
                    cosine = cos_ref[kb : kb + 1, part * 128 : part * 128 + 128]
                    sine = sin_ref[kb : kb + 1, part * 128 : part * 128 + 128]
                    at = pl.ds(pl.multiple_of(kb * ROWS + group * PAIR + index * 8, 8), 8)
                    re = field[at, pl.ds(part * 128, 128)]
                    im = field[at, pl.ds(LANES + part * 128, 128)]
                    values.append((re * cosine + im * sine, im * cosine - re * sine))
                values = dft12(values, 1)
                for block, (first, second) in enumerate(values):
                    lanes = pl.ds(block * LANES + part * 128, 128)
                    orbital = orbital_ref[rows, lanes]
                    applied = first * chosen_ref[step, 0, own, lanes] + second * chosen_ref[step, 1, own, lanes]
                    if step == 0:
                        sums[rows, lanes] = applied
                    else:
                        sums[rows, lanes] = before_ref[rows, lanes] + applied
                    if group == 0:
                        totals[0, own, lanes] = first * orbital
                        totals[1, own, lanes] = second * orbital
                    else:
                        totals[0, own, lanes] += first * orbital
                        totals[1, own, lanes] += second * orbital
        return carry

    lax.fori_loop(0, PAIR // 8, tile, 0)
    core = here_ref[1]
    for offset in range(0, MIDDLE, LANES):
        for where, target in ((core, kept_ref), (1 - core, sent_ref)):
            lanes = pl.ds(pl.multiple_of(where * MIDDLE + offset, 128), LANES)
            first = totals[0, :PLANES, lanes] + totals[0, PLANES:, lanes]
            second = totals[1, :PLANES, lanes] + totals[1, PLANES:, lanes]
            target[:, offset : offset + LANES] = jnp.concatenate([first, second], axis=0)
    if step:
        for block in range(BLOCKS):
            lanes = pl.ds(block * LANES, LANES)
            for band in range(BLOC):
                applied_ref[:, band, lanes] = sums[band * PLANES : band * PLANES + PLANES, lanes]


def pick_kernel(here_ref, owner_ref, picks_ref, orbital_ref, flat_ref, kept_ref, sent_ref):
    core = here_ref[1]
    for offset in range(0, POINTS, LANES):
        lanes = pl.ds(offset, LANES)
        for band in range(BLOC):
            flat_ref[band * PLANES : band * PLANES + PLANES, lanes] = orbital_ref[:, band, lanes]
    for step in range(STEPS):
        mine = owner_ref[step] == here_ref[0]
        for offset in range(0, MIDDLE, LANES):
            for where, target in ((core, kept_ref), (1 - core, sent_ref)):
                lanes = pl.ds(pl.multiple_of(where * MIDDLE + offset, 128), LANES)
                bands = [flat_ref[band * PLANES : band * PLANES + PLANES, lanes] for band in range(BLOC)]
                pair = [pick(bands, picks_ref[step, a]) for a in range(2)]
                target[step * PAIR : step * PAIR + PAIR, offset : offset + LANES] = jnp.where(mine, jnp.concatenate(pair, axis=0), 0.0)


def place_kernel(here_ref, own_ref, other_ref, out_ref):
    core = here_ref[1]
    for step in range(STEPS):
        for offset in range(0, MIDDLE, LANES):
            for where, source in ((core, own_ref), (1 - core, other_ref)):
                lanes = pl.ds(pl.multiple_of(where * MIDDLE + offset, 128), LANES)
                for a in range(2):
                    first = (step * 2 + a) * PLANES
                    out_ref[step, :, a, lanes] = source[first : first + PLANES, offset : offset + LANES]


PARAMS = dict(compiler_params=pltpu.CompilerParams(vmem_limit_bytes=48 * 1024 * 1024))
VMEM = pl.BlockSpec(memory_space=pltpu.VMEM)
SMEM = pl.BlockSpec(memory_space=pltpu.SMEM)
HBM = pl.BlockSpec(memory_space=pltpu.HBM)


def cost(operations, size):
    return pl.CostEstimate(flops=operations, bytes_accessed=size, transcendentals=0)


BOTH_SHAPE = jax.ShapeDtypeStruct((STEPS * PAIR, MIDDLE), jnp.float32)
HALF_SHAPE = jax.ShapeDtypeStruct((PAIR, MIDDLE), jnp.float32)


def pick_orbitals(here, owner, picks, orbitals):
    return pl.pallas_call(
        pick_kernel,
        out_shape=(jax.ShapeDtypeStruct((ROWS, POINTS), jnp.float32),) + (BOTH_SHAPE,) * 2,
        in_specs=[SMEM] * 3 + [VMEM],
        out_specs=(VMEM,) * 3,
        cost_estimate=cost(0, 4_000_000),
        **PARAMS,
    )(here, owner, picks, orbitals)


def place(here, own, other):
    return pl.pallas_call(
        place_kernel,
        out_shape=jax.ShapeDtypeStruct((STEPS, PLANES, 2, POINTS), jnp.float32),
        in_specs=[SMEM] + [VMEM] * 2,
        out_specs=VMEM,
        cost_estimate=cost(0, 2_000_000),
        **PARAMS,
    )(here, own, other)


TABLE_SCRATCH = [
    pltpu.VMEM((2 * LANES, 2 * LANES), jnp.bfloat16),
    pltpu.VMEM((2 * LANES, 2 * LANES), jnp.bfloat16),
    pltpu.SemaphoreType.DMA((2,)),
]


def to_columns(here, orbitals, half, other):
    forward, _, twiddle, _ = tables()
    tall = BLOCKS * ROWS
    return pl.pallas_call(
        forward_kernel,
        out_shape=(
            jax.ShapeDtypeStruct((SLABS, STEPS * ROWS, COLUMNS), jnp.float32),
            jax.ShapeDtypeStruct((STEPS, 2, PAIR, POINTS), jnp.float32),
        ),
        in_specs=[SMEM] + [VMEM] * 5 + [HBM] * 2,
        out_specs=(VMEM, VMEM),
        scratch_shapes=[
            pltpu.VMEM((tall, 2 * LANES), jnp.float32),
            pltpu.VMEM((tall, 2 * LANES), jnp.bfloat16),
            pltpu.VMEM((tall, 2 * LANES), jnp.bfloat16),
        ]
        + TABLE_SCRATCH,
        cost_estimate=cost(12 * tall * (2 * LANES) ** 2, 4_000_000),
        **PARAMS,
    )(here, orbitals, half, other, *twiddle, *forward)


def screened(values, kernel, step):
    _, _, _, along_z = tables()
    return pl.pallas_call(
        functools.partial(middle_kernel, step),
        out_shape=jax.ShapeDtypeStruct((SLABS, ROWS, COLUMNS), jnp.float32),
        in_specs=[VMEM] * 3,
        out_specs=VMEM,
        cost_estimate=cost(2 * 4 * 4 * NZ * 6 * NZ * COLUMNS, 4_000_000),
        **PARAMS,
    )(values, kernel, along_z)


def from_columns(here, values, orbitals, chosen, step, before=None):
    _, inverse, twiddle, _ = tables()
    tall = BLOCKS * ROWS
    first_step = before is None
    applied = (ROWS, POINTS) if first_step else (PLANES, BLOC, POINTS)
    return pl.pallas_call(
        functools.partial(inverse_kernel, step),
        out_shape=(jax.ShapeDtypeStruct(applied, jnp.float32), HALF_SHAPE, HALF_SHAPE),
        in_specs=[SMEM] + [VMEM] * 5 + [HBM] * 2 + ([] if first_step else [VMEM]),
        out_specs=(VMEM,) * 3,
        scratch_shapes=[
            pltpu.VMEM((tall, 2 * LANES), jnp.bfloat16),
            pltpu.VMEM((tall, 2 * LANES), jnp.bfloat16),
            pltpu.VMEM((tall, 2 * LANES), jnp.float32),
            pltpu.VMEM((2, PAIR, POINTS), jnp.float32),
        ]
        + TABLE_SCRATCH
        + ([] if first_step else [pltpu.VMEM((ROWS, POINTS), jnp.float32)]),
        cost_estimate=cost(6 * tall * (2 * LANES) ** 2, 8_000_000),
        **PARAMS,
    )(here, values, orbitals, chosen, *twiddle, *inverse, *(() if first_step else (before,)))


def exchange(columns):
    return lax.all_to_all(columns, ("xh", "y"), split_axis=0, concat_axis=0, tiled=True)


def per_device(orbitals, owner, picks):
    core = lax.axis_index("c")
    group = (lax.axis_index("z") * 2 + lax.axis_index("xl")) * 2 + core
    here = jnp.stack([group, core]).astype(jnp.int32)
    flat, kept, sent = pick_orbitals(here, owner, picks, orbitals.transpose(1, 0, 2))
    half = spread_near(join_far(join_near(join_cores(kept, sent))))
    other = swap(half, "c", 1)
    columns, chosen = to_columns(here, flat, half, other)
    columns, xh, y = tie(columns, lax.axis_index("xh"), lax.axis_index("y"))
    kernel = kernel_columns(xh, y)
    forward = exchange(columns)
    backward = [exchange(screened(forward, kernel, step)) for step in range(STEPS)]
    applied, kept, sent = from_columns(here, backward[0], flat, chosen, 0)
    part = join_near(join_cores(kept, sent))
    last, part = tie(backward[1], part)
    applied, kept, sent = from_columns(here, last, flat, chosen, 1, applied)
    part = jnp.concatenate([part, join_near(join_cores(kept, sent))], axis=0)
    half = spread_near(join_far(part))
    other = swap(half, "c", 1)
    return applied.transpose(1, 0, 2), place(here, half, other).transpose(0, 2, 1, 3)


def solution(mesh):
    fine = Mesh(mesh.devices.reshape(8, 2, 2, 2, 4), ("z", "xl", "c", "xh", "y"))
    band, slab = ("z", "xl", "c"), ("xh", "y")
    in_specs = (P(band, slab, None), P(), P())
    out_specs = (P(band, slab, None), P(None, None, slab, None))
    return jax.shard_map(
        per_device, mesh=fine, in_specs=in_specs, out_specs=out_specs, check_vma=False
    )
```

```python
import functools
import math

import jax
import jax.numpy as jnp
import ml_dtypes
import numpy as np
from jax import lax
from jax.experimental import pallas as pl
from jax.experimental.pallas import tpu as pltpu
from jax.sharding import Mesh, PartitionSpec as P

NX = 48
NY = 96
NZ = 96
BLOC = 4
STEPS = 2
SLABS = 8
PLANES = NZ // SLABS
POINTS = NY * NX
ROWS = BLOC * PLANES
PAIR = 2 * PLANES
BLOCKS = 12
INNER = 8
LANES = INNER * NX
HALF = LANES // 2
COLUMNS = 3 * LANES
MIDDLE = POINTS // 2

length_first = 41.05
length_side = 41.05
length_last = 20.525
omega_screen = 0.106


def swap(x, axis, bit):
    size = lax.axis_size(axis)
    return lax.ppermute(x, axis, [(i, i ^ bit) for i in range(size)])


def near(x, bits):
    z_count, x_count = lax.axis_size("z"), lax.axis_size("xl")
    pairs = [
        (z * x_count + x, (z ^ (bits >> 1)) * x_count + (x ^ (bits & 1)))
        for z in range(z_count)
        for x in range(x_count)
    ]
    return lax.ppermute(x, ("z", "xl"), pairs)


def along(x, distance):
    size = lax.axis_size("z")
    return lax.ppermute(x, "z", [(i, (i + distance) % size) for i in range(size)])


def pick(pieces, index):
    low = jnp.where(index == 0, pieces[0], pieces[1])
    high = jnp.where(index == 2, pieces[2], pieces[3])
    return jnp.where(index < 2, low, high)


def tie(*values):
    return lax.optimization_barrier(values)


def join_cores(kept, sent):
    return kept + swap(sent, "c", 1)


def join_near(half):
    spot = lax.axis_index("z") % 2 * 2 + lax.axis_index("xl")
    width = half.shape[1] // 4
    quarters = [half[:, i * width : (i + 1) * width] for i in range(4)]
    arrived = [near(pick(quarters, spot ^ bits), bits) for bits in (1, 2, 3)]
    return pick(quarters, spot) + arrived[0] + arrived[1] + arrived[2]


def join_far(part):
    arrived = [along(part, distance) for distance in (2, 4, 6)]
    return part + arrived[0] + arrived[1] + arrived[2]


def spread_near(part):
    spot = lax.axis_index("z") % 2 * 2 + lax.axis_index("xl")
    quarters = [part] + [near(part, bits) for bits in (1, 2, 3)]
    return jnp.concatenate([pick(quarters, spot ^ i) for i in range(4)], axis=1)


def frequency(counter, length):
    return jnp.where(counter <= length // 2, counter, counter - length).astype(jnp.float32)


def coulomb_kernel(freq_z, freq_y, freq_x):
    squared = (
        (2.0 * math.pi / length_first * freq_z) ** 2
        + (2.0 * math.pi / length_side * freq_y) ** 2
        + (2.0 * math.pi / length_last * freq_x) ** 2
    )
    safe = jnp.where(squared > 0, squared, 1.0)
    screened = -4.0 * math.pi * jnp.expm1(-squared / (4.0 * omega_screen**2)) / safe
    return jnp.where(squared > 0, screened, math.pi / omega_screen**2)


def kernel_columns(xh, y):
    row = jnp.arange(2 * NZ)[:, None]
    lane = jnp.arange(COLUMNS)[None, :]
    kz = row // PAIR * PLANES + row % PLANES
    kb = 3 * y + lane // LANES
    kk = 4 * xh + lane % HALF // NX
    return coulomb_kernel(
        frequency(kz, NZ), frequency(kb + BLOCKS * kk, NY), frequency(lane % NX, NX)
    ) * (1.0 / (NX * NY * NZ))


def split_table(table):
    high = table.astype(ml_dtypes.bfloat16)
    low = (table - high.astype(np.float64)).astype(ml_dtypes.bfloat16)
    return high, low


@functools.cache
def tables():
    inner, x = np.divmod(np.arange(LANES), NX)
    angle = -2.0 * np.pi * (
        (inner[:, None] * inner[None, :] % INNER) / INNER + (x[:, None] * x[None, :] % NX) / NX
    )
    real, imag = np.cos(angle), np.sin(angle)
    forward = np.zeros((2, LANES, 2, 2, HALF))
    inverse = np.zeros((2, 2, HALF, 2, LANES))
    for half in range(2):
        part = slice(half * HALF, (half + 1) * HALF)
        forward[0, :, half, 0], forward[1, :, half, 0] = real[:, part], -imag[:, part]
        forward[0, :, half, 1], forward[1, :, half, 1] = imag[:, part], real[:, part]
        inverse[half, 0, :, 0], inverse[half, 1, :, 0] = real[part], imag[part]
        inverse[half, 0, :, 1], inverse[half, 1, :, 1] = -imag[part], real[part]
    forward = split_table(forward.reshape(2 * LANES, 2 * LANES))
    inverse = split_table(inverse.reshape(2 * LANES, 2 * LANES))
    turn = -2.0 * np.pi / NY * (np.arange(BLOCKS)[:, None] * inner[None, :] % NY)
    twiddle = np.cos(turn).astype(np.float32), np.sin(turn).astype(np.float32)
    slab, rest = np.divmod(np.arange(2 * NZ), PAIR)
    band, plane = np.divmod(rest, PLANES)
    z = slab * PLANES + plane
    same = band[:, None] == band[None, :]
    angle = 2.0 * np.pi / NZ * (z[:, None] * z[None, :] % NZ)
    stacked = np.concatenate([np.where(same, np.cos(angle), 0), np.where(same, np.sin(angle), 0)])
    high, low = split_table(stacked)
    along_z = np.concatenate([high, high, low], axis=1)
    return forward, inverse, twiddle, along_z


def split(x):
    high = x.astype(jnp.bfloat16)
    return high, (x - high.astype(jnp.float32)).astype(jnp.bfloat16)


def dot(a, b):
    return lax.dot_general(a, b, (((1,), (0,)), ((), ())), preferred_element_type=jnp.float32)


def dft12(values, sign):
    def turn(value):
        re, im = value
        return (-im, re) if sign > 0 else (im, -re)

    def add(a, b):
        return a[0] + b[0], a[1] + b[1]

    def sub(a, b):
        return a[0] - b[0], a[1] - b[1]

    quarter = []
    for n1 in range(3):
        a = [values[(4 * n1 + 3 * n2) % 12] for n2 in range(4)]
        even, odd = add(a[0], a[2]), add(a[1], a[3])
        left, right = sub(a[0], a[2]), turn(sub(a[1], a[3]))
        quarter.append([add(even, odd), add(left, right), sub(even, odd), sub(left, right)])
    result = [None] * 12
    for k4 in range(4):
        b = [quarter[n1][k4] for n1 in range(3)]
        total = add(b[1], b[2])
        difference = sub(b[1], b[2])
        middle = (b[0][0] - 0.5 * total[0], b[0][1] - 0.5 * total[1])
        scale = math.sqrt(0.75)
        side = turn((scale * difference[0], scale * difference[1]))
        for k3, value in enumerate((add(b[0], total), add(middle, side), sub(middle, side))):
            where = next(k for k in range(12) if k % 3 == k3 and k % 4 == k4)
            result[where] = value
    return result


def spot_of(here_ref, piece, direction):
    return (here_ref[2] ^ (piece // 4)) * 4 + (here_ref[3] + direction * (piece % 4)) % 4


def forward_kernel(step, whole, here_ref, orbital_ref, half_ref, other_ref, cos_ref, sin_ref, high_source, low_source, *rest):
    count = 1 if whole else SLABS
    outs, chosen_ref = rest[:count], rest[count]
    field, field_high, field_low, staged, high_ref, low_ref, loaded = rest[count + 1 :]
    if whole:
        staged = outs[0]
    loads = [
        pltpu.make_async_copy(source, target, loaded.at[index])
        for index, (source, target) in enumerate(((high_source, high_ref), (low_source, low_ref)))
    ]
    for load in loads:
        load.start()
    core = here_ref[1]
    for offset in range(0, MIDDLE, LANES):
        for where, source in ((core, half_ref), (1 - core, other_ref)):
            lanes = pl.ds(pl.multiple_of(where * MIDDLE + offset, 128), LANES)
            for a in range(2):
                first = (step * 2 + a) * PLANES
                rows = source[first : first + PLANES, offset : offset + LANES]
                chosen_ref[a, :, lanes] = jnp.concatenate([rows, rows], axis=0)


    def tile(index, carry):
        for group in range(2):
            for part in range(3):
                rows = pl.ds(pl.multiple_of(group * PAIR + index * 8, 8), 8)
                own = pl.ds(pl.multiple_of(index * 8, 8), 8)
                values = []
                for block in range(BLOCKS):
                    lanes = pl.ds(block * LANES + part * 128, 128)
                    orbital = orbital_ref[rows, lanes]
                    values.append(
                        (orbital * chosen_ref[0, own, lanes], orbital * chosen_ref[1, own, lanes])
                    )
                values = dft12(values, -1)
                for kb, (re, im) in enumerate(values):
                    cosine = cos_ref[kb : kb + 1, part * 128 : part * 128 + 128]
                    sine = sin_ref[kb : kb + 1, part * 128 : part * 128 + 128]
                    to = pl.ds(pl.multiple_of(kb * ROWS + group * PAIR + index * 8, 8), 8)
                    field[to, pl.ds(part * 128, 128)] = re * cosine - im * sine
                    field[to, pl.ds(LANES + part * 128, 128)] = re * sine + im * cosine
        return carry

    lax.fori_loop(0, PAIR // 8, tile, 0)
    field_high[...], field_low[...] = split(field[...])
    for load in loads:
        load.wait()
    for piece in range(3):
        lanes = pl.ds(piece * 256, 256)
        high = high_ref[:, lanes]
        result = dot(field_high[...], high) + dot(field_low[...], high) + dot(field_high[...], low_ref[:, lanes])
        for part in range(2):
            half, offset = divmod(2 * piece + part, 3)
            for kb in range(BLOCKS):
                column, turn = divmod(kb, 3)
                staged[
                    half * 4 + column, :, pl.ds(turn * LANES + offset * 128, 128)
                ] = result[kb * ROWS : kb * ROWS + ROWS, part * 128 : part * 128 + 128]
    for piece, out_ref in enumerate(() if whole else outs):
        out_ref[...] = staged[spot_of(here_ref, piece, 1)]


def middle_kernel(whole, here_ref, *refs):
    count = 1 if whole else SLABS
    values, kernel_ref, table_ref = refs[:count], refs[count], refs[count + 1]
    outs, staged = refs[count + 2 : -1], refs[-1]
    source = values[0] if whole else staged
    target = outs[0] if whole else staged
    for piece, value_ref in enumerate(() if whole else values):
        staged[spot_of(here_ref, piece, -1)] = value_ref[...]
    imaginary = lax.broadcasted_iota(jnp.int32, (2 * NZ, LANES), 1) >= HALF

    def swapped(x):
        return jnp.concatenate([x[:, HALF:], x[:, :HALF]], axis=1)

    def transform(x, sign):
        high, low = split(x)
        both = dot(table_ref[...], jnp.concatenate([high, low, high], axis=0))
        cosine, sine = both[: 2 * NZ], swapped(both[2 * NZ :])
        return cosine + jnp.where(imaginary, -sign * sine, sign * sine)

    for group in range(ROWS // PAIR):
        own = slice(group * PAIR, group * PAIR + PAIR)
        for turn in range(3):
            lanes = slice(turn * LANES, turn * LANES + LANES)
            x = jnp.concatenate([source[slab, own, lanes] for slab in range(SLABS)], axis=0)
            x = transform(x, 1.0) * kernel_ref[:, lanes]
            x = transform(x, -1.0)
            for slab in range(SLABS):
                target[slab, own, lanes] = x[slab * PAIR : slab * PAIR + PAIR]
    for piece, out_ref in enumerate(() if whole else outs):
        out_ref[...] = staged[spot_of(here_ref, piece, 1)]


def inverse_kernel(
    step, whole, here_ref, orbital_ref, chosen_ref, cos_ref, sin_ref, high_source, low_source, *rest
):
    count = 1 if whole else SLABS
    values, rest = rest[:count], rest[count:]
    if step == 0:
        applied_ref, kept_ref, sent_ref, field_high, field_low, field, totals, staged, high_ref, low_ref, loaded = rest
        sums = applied_ref
    else:
        before_ref, applied_ref, kept_ref, sent_ref, field_high, field_low, field, totals, staged, high_ref, low_ref, loaded, sums = rest
    loads = [
        pltpu.make_async_copy(source, target, loaded.at[index])
        for index, (source, target) in enumerate(((high_source, high_ref), (low_source, low_ref)))
    ]
    for load in loads:
        load.start()
    if whole:
        staged = values[0]
    for piece, value_ref in enumerate(() if whole else values):
        staged[spot_of(here_ref, piece, -1)] = value_ref[...]
    for kb in range(BLOCKS):
        column, turn = divmod(kb, 3)
        for half in range(2):
            x = staged[half * 4 + column, :, pl.ds(turn * LANES, LANES)]
            high, low = split(x)
            field_high[kb * ROWS : kb * ROWS + ROWS, half * LANES : half * LANES + LANES] = high
            field_low[kb * ROWS : kb * ROWS + ROWS, half * LANES : half * LANES + LANES] = low
    for load in loads:
        load.wait()
    for piece in range(3):
        lanes = pl.ds(piece * 256, 256)
        high = high_ref[:, lanes]
        field[:, lanes] = (
            dot(field_high[...], high) + dot(field_low[...], high) + dot(field_high[...], low_ref[:, lanes])
        )

    def tile(index, carry):
        own = pl.ds(pl.multiple_of(index * 8, 8), 8)
        for part in range(3):
            for group in range(2):
                rows = pl.ds(pl.multiple_of(group * PAIR + index * 8, 8), 8)
                values = []
                for kb in range(BLOCKS):
                    cosine = cos_ref[kb : kb + 1, part * 128 : part * 128 + 128]
                    sine = sin_ref[kb : kb + 1, part * 128 : part * 128 + 128]
                    at = pl.ds(pl.multiple_of(kb * ROWS + group * PAIR + index * 8, 8), 8)
                    re = field[at, pl.ds(part * 128, 128)]
                    im = field[at, pl.ds(LANES + part * 128, 128)]
                    values.append((re * cosine + im * sine, im * cosine - re * sine))
                values = dft12(values, 1)
                for block, (first, second) in enumerate(values):
                    lanes = pl.ds(block * LANES + part * 128, 128)
                    orbital = orbital_ref[rows, lanes]
                    applied = first * chosen_ref[0, own, lanes] + second * chosen_ref[1, own, lanes]
                    if step == 0:
                        sums[rows, lanes] = applied
                    else:
                        sums[rows, lanes] = before_ref[rows, lanes] + applied
                    if group == 0:
                        totals[0, own, lanes] = first * orbital
                        totals[1, own, lanes] = second * orbital
                    else:
                        totals[0, own, lanes] += first * orbital
                        totals[1, own, lanes] += second * orbital
        return carry

    lax.fori_loop(0, PAIR // 8, tile, 0)
    core = here_ref[1]
    for offset in range(0, MIDDLE, LANES):
        for where, target in ((core, kept_ref), (1 - core, sent_ref)):
            lanes = pl.ds(pl.multiple_of(where * MIDDLE + offset, 128), LANES)
            first = totals[0, :PLANES, lanes] + totals[0, PLANES:, lanes]
            second = totals[1, :PLANES, lanes] + totals[1, PLANES:, lanes]
            target[:, offset : offset + LANES] = jnp.concatenate([first, second], axis=0)
    if step:
        for block in range(BLOCKS):
            lanes = pl.ds(block * LANES, LANES)
            for band in range(BLOC):
                applied_ref[:, band, lanes] = sums[band * PLANES : band * PLANES + PLANES, lanes]


def pick_kernel(here_ref, owner_ref, picks_ref, orbital_ref, flat_ref, kept_ref, sent_ref):
    core = here_ref[1]
    for offset in range(0, POINTS, LANES):
        lanes = pl.ds(offset, LANES)
        for band in range(BLOC):
            flat_ref[band * PLANES : band * PLANES + PLANES, lanes] = orbital_ref[:, band, lanes]
    for step in range(STEPS):
        mine = owner_ref[step] == here_ref[0]
        for offset in range(0, MIDDLE, LANES):
            for where, target in ((core, kept_ref), (1 - core, sent_ref)):
                lanes = pl.ds(pl.multiple_of(where * MIDDLE + offset, 128), LANES)
                bands = [flat_ref[band * PLANES : band * PLANES + PLANES, lanes] for band in range(BLOC)]
                pair = [pick(bands, picks_ref[step, a]) for a in range(2)]
                target[step * PAIR : step * PAIR + PAIR, offset : offset + LANES] = jnp.where(mine, jnp.concatenate(pair, axis=0), 0.0)


def place_kernel(here_ref, own_ref, other_ref, out_ref):
    core = here_ref[1]
    for step in range(STEPS):
        for offset in range(0, MIDDLE, LANES):
            for where, source in ((core, own_ref), (1 - core, other_ref)):
                lanes = pl.ds(pl.multiple_of(where * MIDDLE + offset, 128), LANES)
                for a in range(2):
                    first = (step * 2 + a) * PLANES
                    out_ref[step, :, a, lanes] = source[first : first + PLANES, offset : offset + LANES]


PARAMS = dict(compiler_params=pltpu.CompilerParams(vmem_limit_bytes=48 * 1024 * 1024))
VMEM = pl.BlockSpec(memory_space=pltpu.VMEM)
SMEM = pl.BlockSpec(memory_space=pltpu.SMEM)
HBM = pl.BlockSpec(memory_space=pltpu.HBM)


def cost(operations, size):
    return pl.CostEstimate(flops=operations, bytes_accessed=size, transcendentals=0)


BOTH_SHAPE = jax.ShapeDtypeStruct((STEPS * PAIR, MIDDLE), jnp.float32)
HALF_SHAPE = jax.ShapeDtypeStruct((PAIR, MIDDLE), jnp.float32)


def pick_orbitals(here, owner, picks, orbitals):
    return pl.pallas_call(
        pick_kernel,
        out_shape=(jax.ShapeDtypeStruct((ROWS, POINTS), jnp.float32),) + (BOTH_SHAPE,) * 2,
        in_specs=[SMEM] * 3 + [VMEM],
        out_specs=(VMEM,) * 3,
        cost_estimate=cost(0, 4_000_000),
        **PARAMS,
    )(here, owner, picks, orbitals)


def place(here, own, other):
    return pl.pallas_call(
        place_kernel,
        out_shape=jax.ShapeDtypeStruct((STEPS, PLANES, 2, POINTS), jnp.float32),
        in_specs=[SMEM] + [VMEM] * 2,
        out_specs=VMEM,
        cost_estimate=cost(0, 2_000_000),
        **PARAMS,
    )(here, own, other)


TABLE_SCRATCH = [
    pltpu.VMEM((2 * LANES, 2 * LANES), jnp.bfloat16),
    pltpu.VMEM((2 * LANES, 2 * LANES), jnp.bfloat16),
    pltpu.SemaphoreType.DMA((2,)),
]


PIECE = jax.ShapeDtypeStruct((ROWS, COLUMNS), jnp.float32)
WHOLE = jax.ShapeDtypeStruct((SLABS, ROWS, COLUMNS), jnp.float32)
STAGED = pltpu.VMEM((SLABS, ROWS, COLUMNS), jnp.float32)


def to_columns(here, orbitals, half, other, step, whole):
    shapes = (WHOLE,) if whole else (PIECE,) * SLABS
    forward, _, twiddle, _ = tables()
    tall = BLOCKS * ROWS
    *columns, chosen = pl.pallas_call(
        functools.partial(forward_kernel, step, whole),
        out_shape=shapes + (jax.ShapeDtypeStruct((2, PAIR, POINTS), jnp.float32),),
        in_specs=[SMEM] + [VMEM] * 5 + [HBM] * 2,
        out_specs=(VMEM,) * (len(shapes) + 1),
        scratch_shapes=[
            pltpu.VMEM((tall, 2 * LANES), jnp.float32),
            pltpu.VMEM((tall, 2 * LANES), jnp.bfloat16),
            pltpu.VMEM((tall, 2 * LANES), jnp.bfloat16),
            STAGED,
        ]
        + TABLE_SCRATCH,
        cost_estimate=cost(6 * tall * (2 * LANES) ** 2, 4_000_000),
        **PARAMS,
    )(here, orbitals, half, other, *twiddle, *forward)
    return columns, chosen


def screened(here, values, kernel):
    _, _, _, along_z = tables()
    whole = len(values) == 1
    shapes = (WHOLE,) if whole else (PIECE,) * SLABS
    return pl.pallas_call(
        functools.partial(middle_kernel, whole),
        out_shape=shapes,
        in_specs=[SMEM] + [VMEM] * (len(values) + 2),
        out_specs=(VMEM,) * len(shapes),
        scratch_shapes=[STAGED],
        cost_estimate=cost(2 * 4 * 4 * NZ * 6 * NZ * COLUMNS, 4_000_000),
        **PARAMS,
    )(here, *values, kernel, along_z)


def from_columns(here, values, orbitals, chosen, step, before=None):
    _, inverse, twiddle, _ = tables()
    tall = BLOCKS * ROWS
    first_step = before is None
    applied = (ROWS, POINTS) if first_step else (PLANES, BLOC, POINTS)
    return pl.pallas_call(
        functools.partial(inverse_kernel, step, len(values) == 1),
        out_shape=(jax.ShapeDtypeStruct(applied, jnp.float32), HALF_SHAPE, HALF_SHAPE),
        in_specs=[SMEM] + [VMEM] * 4 + [HBM] * 2 + [VMEM] * (len(values) + (0 if first_step else 1)),
        out_specs=(VMEM,) * 3,
        scratch_shapes=[
            pltpu.VMEM((tall, 2 * LANES), jnp.bfloat16),
            pltpu.VMEM((tall, 2 * LANES), jnp.bfloat16),
            pltpu.VMEM((tall, 2 * LANES), jnp.float32),
            pltpu.VMEM((2, PAIR, POINTS), jnp.float32),
            STAGED,
        ]
        + TABLE_SCRATCH
        + ([] if first_step else [pltpu.VMEM((ROWS, POINTS), jnp.float32)]),
        cost_estimate=cost(6 * tall * (2 * LANES) ** 2, 8_000_000),
        **PARAMS,
    )(here, orbitals, chosen, *twiddle, *inverse, *values, *(() if first_step else (before,)))


def exchange(pieces):
    if len(pieces) == 1:
        return [lax.all_to_all(pieces[0], ("xh", "y"), split_axis=0, concat_axis=0, tiled=True)]
    moved = [pieces[0]]
    for piece in range(1, SLABS):
        pairs = [
            (x * 4 + y, (x ^ (piece // 4)) * 4 + (y + piece % 4) % 4) for x in range(2) for y in range(4)
        ]
        moved.append(lax.ppermute(pieces[piece], ("xh", "y"), pairs))
    return moved


def per_device(orbitals, owner, picks):
    core, xh, y = lax.axis_index("c"), lax.axis_index("xh"), lax.axis_index("y")
    group = (lax.axis_index("z") * 2 + lax.axis_index("xl")) * 2 + core
    here = jnp.stack([group, core, xh, y]).astype(jnp.int32)
    flat, kept, sent = pick_orbitals(here, owner, picks, orbitals.transpose(1, 0, 2))
    half = spread_near(join_far(join_near(join_cores(kept, sent))))
    other = swap(half, "c", 1)
    columns0, chosen0 = to_columns(here, flat, half, other, 0, True)
    forward0 = exchange(columns0)
    half, _ = tie(half, chosen0)
    columns1, chosen1 = to_columns(here, flat, half, other, 1, True)
    first, xh, y = tie(columns1[0], xh, y)
    kernel = kernel_columns(xh, y)
    forward1 = exchange([first] + columns1[1:])
    backward0 = exchange(screened(here, forward0, kernel))
    backward1 = exchange(screened(here, forward1, kernel))
    applied, kept, sent = from_columns(here, backward0, flat, chosen0, 0)
    part = join_near(join_cores(kept, sent))
    last, part = tie(backward1[0], part)
    applied, kept, sent = from_columns(here, [last] + backward1[1:], flat, chosen1, 1, applied)
    part = jnp.concatenate([part, join_near(join_cores(kept, sent))], axis=0)
    half = spread_near(join_far(part))
    other = swap(half, "c", 1)
    return applied.transpose(1, 0, 2), place(here, half, other).transpose(0, 2, 1, 3)


def solution(mesh):
    fine = Mesh(mesh.devices.reshape(8, 2, 2, 2, 4), ("z", "xl", "c", "xh", "y"))
    band, slab = ("z", "xl", "c"), ("xh", "y")
    in_specs = (P(band, slab, None), P(), P())
    out_specs = (P(band, slab, None), P(None, None, slab, None))
    return jax.shard_map(
        per_device, mesh=fine, in_specs=in_specs, out_specs=out_specs, check_vma=False
    )
```

```python
import functools
import math

import jax
import jax.numpy as jnp
import ml_dtypes
import numpy as np
from jax import lax
from jax.experimental import pallas as pl
from jax.experimental.pallas import tpu as pltpu
from jax.sharding import Mesh, PartitionSpec as P

NX = 48
NY = 96
NZ = 96
BLOC = 4
STEPS = 2
SLABS = 8
PLANES = NZ // SLABS
POINTS = NY * NX
ROWS = BLOC * PLANES
PAIR = 2 * PLANES
BLOCKS = 12
INNER = 8
LANES = INNER * NX
HALF = LANES // 2
COLUMNS = 3 * LANES
MIDDLE = POINTS // 2

length_first = 41.05
length_side = 41.05
length_last = 20.525
omega_screen = 0.106


def swap(x, axis, bit):
    size = lax.axis_size(axis)
    return lax.ppermute(x, axis, [(i, i ^ bit) for i in range(size)])


def near(x, bits):
    z_count, x_count = lax.axis_size("z"), lax.axis_size("xl")
    pairs = [
        (z * x_count + x, (z ^ (bits >> 1)) * x_count + (x ^ (bits & 1)))
        for z in range(z_count)
        for x in range(x_count)
    ]
    return lax.ppermute(x, ("z", "xl"), pairs)


def along(x, distance):
    size = lax.axis_size("z")
    return lax.ppermute(x, "z", [(i, (i + distance) % size) for i in range(size)])


def pick(pieces, index):
    low = jnp.where(index == 0, pieces[0], pieces[1])
    high = jnp.where(index == 2, pieces[2], pieces[3])
    return jnp.where(index < 2, low, high)


def tie(*values):
    return lax.optimization_barrier(values)


def join_cores(kept, sent):
    return kept + swap(sent, "c", 1)


def join_near(half):
    spot = lax.axis_index("z") % 2 * 2 + lax.axis_index("xl")
    width = half.shape[1] // 4
    quarters = [half[:, i * width : (i + 1) * width] for i in range(4)]
    arrived = [near(pick(quarters, spot ^ bits), bits) for bits in (1, 2, 3)]
    return pick(quarters, spot) + arrived[0] + arrived[1] + arrived[2]


def join_far(part):
    above, below, across = [along(part, distance) for distance in (6, 2, 4)]
    return (part + across) + (below + above)


def spread_near(part):
    spot = lax.axis_index("z") % 2 * 2 + lax.axis_index("xl")
    quarters = [part] + [near(part, bits) for bits in (1, 2, 3)]
    return jnp.concatenate([pick(quarters, spot ^ i) for i in range(4)], axis=1)


def frequency(counter, length):
    return jnp.where(counter <= length // 2, counter, counter - length).astype(jnp.float32)


def coulomb_kernel(freq_z, freq_y, freq_x):
    squared = (
        (2.0 * math.pi / length_first * freq_z) ** 2
        + (2.0 * math.pi / length_side * freq_y) ** 2
        + (2.0 * math.pi / length_last * freq_x) ** 2
    )
    safe = jnp.where(squared > 0, squared, 1.0)
    screened = -4.0 * math.pi * jnp.expm1(-squared / (4.0 * omega_screen**2)) / safe
    return jnp.where(squared > 0, screened, math.pi / omega_screen**2)


def kernel_columns(xh, y):
    row = jnp.arange(2 * NZ)[:, None]
    lane = jnp.arange(COLUMNS)[None, :]
    kz = row // PAIR * PLANES + row % PLANES
    kb = 3 * y + lane // LANES
    kk = 4 * xh + lane % HALF // NX
    return coulomb_kernel(
        frequency(kz, NZ), frequency(kb + BLOCKS * kk, NY), frequency(lane % NX, NX)
    ) * (1.0 / (NX * NY * NZ))


def split_table(table):
    high = table.astype(ml_dtypes.bfloat16)
    low = (table - high.astype(np.float64)).astype(ml_dtypes.bfloat16)
    return high, low


@functools.cache
def tables():
    inner, x = np.divmod(np.arange(LANES), NX)
    angle = -2.0 * np.pi * (
        (inner[:, None] * inner[None, :] % INNER) / INNER + (x[:, None] * x[None, :] % NX) / NX
    )
    real, imag = np.cos(angle), np.sin(angle)
    forward = np.zeros((2, LANES, 2, 2, HALF))
    inverse = np.zeros((2, 2, HALF, 2, LANES))
    for half in range(2):
        part = slice(half * HALF, (half + 1) * HALF)
        forward[0, :, half, 0], forward[1, :, half, 0] = real[:, part], -imag[:, part]
        forward[0, :, half, 1], forward[1, :, half, 1] = imag[:, part], real[:, part]
        inverse[half, 0, :, 0], inverse[half, 1, :, 0] = real[part], imag[part]
        inverse[half, 0, :, 1], inverse[half, 1, :, 1] = -imag[part], real[part]
    forward = split_table(forward.reshape(2 * LANES, 2 * LANES))
    inverse = split_table(inverse.reshape(2 * LANES, 2 * LANES))
    turn = -2.0 * np.pi / NY * (np.arange(BLOCKS)[:, None] * inner[None, :] % NY)
    twiddle = np.cos(turn).astype(np.float32), np.sin(turn).astype(np.float32)
    slab, rest = np.divmod(np.arange(2 * NZ), PAIR)
    band, plane = np.divmod(rest, PLANES)
    z = slab * PLANES + plane
    same = band[:, None] == band[None, :]
    angle = 2.0 * np.pi / NZ * (z[:, None] * z[None, :] % NZ)
    stacked = np.concatenate([np.where(same, np.cos(angle), 0), np.where(same, np.sin(angle), 0)])
    high, low = split_table(stacked)
    along_z = np.concatenate([high, high, low], axis=1)
    return forward, inverse, twiddle, along_z


def split(x):
    high = x.astype(jnp.bfloat16)
    return high, (x - high.astype(jnp.float32)).astype(jnp.bfloat16)


def dot(a, b):
    return lax.dot_general(a, b, (((1,), (0,)), ((), ())), preferred_element_type=jnp.float32)


def dft12(values, sign):
    def turn(value):
        re, im = value
        return (-im, re) if sign > 0 else (im, -re)

    def add(a, b):
        return a[0] + b[0], a[1] + b[1]

    def sub(a, b):
        return a[0] - b[0], a[1] - b[1]

    quarter = []
    for n1 in range(3):
        a = [values[(4 * n1 + 3 * n2) % 12] for n2 in range(4)]
        even, odd = add(a[0], a[2]), add(a[1], a[3])
        left, right = sub(a[0], a[2]), turn(sub(a[1], a[3]))
        quarter.append([add(even, odd), add(left, right), sub(even, odd), sub(left, right)])
    result = [None] * 12
    for k4 in range(4):
        b = [quarter[n1][k4] for n1 in range(3)]
        total = add(b[1], b[2])
        difference = sub(b[1], b[2])
        middle = (b[0][0] - 0.5 * total[0], b[0][1] - 0.5 * total[1])
        scale = math.sqrt(0.75)
        side = turn((scale * difference[0], scale * difference[1]))
        for k3, value in enumerate((add(b[0], total), add(middle, side), sub(middle, side))):
            where = next(k for k in range(12) if k % 3 == k3 and k % 4 == k4)
            result[where] = value
    return result


def spot_of(here_ref, piece, direction):
    return (here_ref[2] ^ (piece // 4)) * 4 + (here_ref[3] + direction * (piece % 4)) % 4


def forward_kernel(step, whole, here_ref, orbital_ref, half_ref, other_ref, cos_ref, sin_ref, high_source, low_source, *rest):
    count = 1 if whole else SLABS
    outs, chosen_ref = rest[:count], rest[count]
    field, field_high, field_low, staged, high_ref, low_ref, loaded = rest[count + 1 :]
    if whole:
        staged = outs[0]
    loads = [
        pltpu.make_async_copy(source, target, loaded.at[index])
        for index, (source, target) in enumerate(((high_source, high_ref), (low_source, low_ref)))
    ]
    for load in loads:
        load.start()
    core = here_ref[1]
    for offset in range(0, MIDDLE, LANES):
        for where, source in ((core, half_ref), (1 - core, other_ref)):
            lanes = pl.ds(pl.multiple_of(where * MIDDLE + offset, 128), LANES)
            for a in range(2):
                first = (step * 2 + a) * PLANES
                rows = source[first : first + PLANES, offset : offset + LANES]
                chosen_ref[a, :, lanes] = jnp.concatenate([rows, rows], axis=0)


    def tile(index, carry):
        for group in range(2):
            for part in range(3):
                rows = pl.ds(pl.multiple_of(group * PAIR + index * 8, 8), 8)
                own = pl.ds(pl.multiple_of(index * 8, 8), 8)
                values = []
                for block in range(BLOCKS):
                    lanes = pl.ds(block * LANES + part * 128, 128)
                    orbital = orbital_ref[rows, lanes]
                    values.append(
                        (orbital * chosen_ref[0, own, lanes], orbital * chosen_ref[1, own, lanes])
                    )
                values = dft12(values, -1)
                for kb, (re, im) in enumerate(values):
                    cosine = cos_ref[kb : kb + 1, part * 128 : part * 128 + 128]
                    sine = sin_ref[kb : kb + 1, part * 128 : part * 128 + 128]
                    to = pl.ds(pl.multiple_of(kb * ROWS + group * PAIR + index * 8, 8), 8)
                    field[to, pl.ds(part * 128, 128)] = re * cosine - im * sine
                    field[to, pl.ds(LANES + part * 128, 128)] = re * sine + im * cosine
        return carry

    lax.fori_loop(0, PAIR // 8, tile, 0)
    field_high[...], field_low[...] = split(field[...])
    for load in loads:
        load.wait()
    for piece in range(3):
        lanes = pl.ds(piece * 256, 256)
        high = high_ref[:, lanes]
        result = dot(field_high[...], high) + dot(field_low[...], high) + dot(field_high[...], low_ref[:, lanes])
        for part in range(2):
            half, offset = divmod(2 * piece + part, 3)
            for kb in range(BLOCKS):
                column, turn = divmod(kb, 3)
                staged[
                    half * 4 + column, :, pl.ds(turn * LANES + offset * 128, 128)
                ] = result[kb * ROWS : kb * ROWS + ROWS, part * 128 : part * 128 + 128]
    for piece, out_ref in enumerate(() if whole else outs):
        out_ref[...] = staged[spot_of(here_ref, piece, 1)]


def middle_kernel(whole, here_ref, *refs):
    count = 1 if whole else SLABS
    values, kernel_ref, table_ref = refs[:count], refs[count], refs[count + 1]
    outs, staged = refs[count + 2 : -1], refs[-1]
    source = values[0] if whole else staged
    target = outs[0] if whole else staged
    for piece, value_ref in enumerate(() if whole else values):
        staged[spot_of(here_ref, piece, -1)] = value_ref[...]
    imaginary = lax.broadcasted_iota(jnp.int32, (2 * NZ, LANES), 1) >= HALF

    def swapped(x):
        return jnp.concatenate([x[:, HALF:], x[:, :HALF]], axis=1)

    def transform(x, sign):
        high, low = split(x)
        both = dot(table_ref[...], jnp.concatenate([high, low, high], axis=0))
        cosine, sine = both[: 2 * NZ], swapped(both[2 * NZ :])
        return cosine + jnp.where(imaginary, -sign * sine, sign * sine)

    for group in range(ROWS // PAIR):
        own = slice(group * PAIR, group * PAIR + PAIR)
        for turn in range(3):
            lanes = slice(turn * LANES, turn * LANES + LANES)
            x = jnp.concatenate([source[slab, own, lanes] for slab in range(SLABS)], axis=0)
            x = transform(x, 1.0) * kernel_ref[:, lanes]
            x = transform(x, -1.0)
            for slab in range(SLABS):
                target[slab, own, lanes] = x[slab * PAIR : slab * PAIR + PAIR]
    for piece, out_ref in enumerate(() if whole else outs):
        out_ref[...] = staged[spot_of(here_ref, piece, 1)]


def inverse_kernel(
    step, whole, here_ref, orbital_ref, chosen_ref, cos_ref, sin_ref, high_source, low_source, *rest
):
    count = 1 if whole else SLABS
    values, rest = rest[:count], rest[count:]
    if step == 0:
        applied_ref, kept_ref, sent_ref, field_high, field_low, field, totals, staged, high_ref, low_ref, loaded = rest
        sums = applied_ref
    else:
        before_ref, applied_ref, kept_ref, sent_ref, field_high, field_low, field, totals, staged, high_ref, low_ref, loaded, sums = rest
    loads = [
        pltpu.make_async_copy(source, target, loaded.at[index])
        for index, (source, target) in enumerate(((high_source, high_ref), (low_source, low_ref)))
    ]
    for load in loads:
        load.start()
    if whole:
        staged = values[0]
    for piece, value_ref in enumerate(() if whole else values):
        staged[spot_of(here_ref, piece, -1)] = value_ref[...]
    for kb in range(BLOCKS):
        column, turn = divmod(kb, 3)
        for half in range(2):
            x = staged[half * 4 + column, :, pl.ds(turn * LANES, LANES)]
            high, low = split(x)
            field_high[kb * ROWS : kb * ROWS + ROWS, half * LANES : half * LANES + LANES] = high
            field_low[kb * ROWS : kb * ROWS + ROWS, half * LANES : half * LANES + LANES] = low
    for load in loads:
        load.wait()
    for piece in range(3):
        lanes = pl.ds(piece * 256, 256)
        high = high_ref[:, lanes]
        field[:, lanes] = (
            dot(field_high[...], high) + dot(field_low[...], high) + dot(field_high[...], low_ref[:, lanes])
        )

    def tile(index, carry):
        own = pl.ds(pl.multiple_of(index * 8, 8), 8)
        for part in range(3):
            for group in range(2):
                rows = pl.ds(pl.multiple_of(group * PAIR + index * 8, 8), 8)
                values = []
                for kb in range(BLOCKS):
                    cosine = cos_ref[kb : kb + 1, part * 128 : part * 128 + 128]
                    sine = sin_ref[kb : kb + 1, part * 128 : part * 128 + 128]
                    at = pl.ds(pl.multiple_of(kb * ROWS + group * PAIR + index * 8, 8), 8)
                    re = field[at, pl.ds(part * 128, 128)]
                    im = field[at, pl.ds(LANES + part * 128, 128)]
                    values.append((re * cosine + im * sine, im * cosine - re * sine))
                values = dft12(values, 1)
                for block, (first, second) in enumerate(values):
                    lanes = pl.ds(block * LANES + part * 128, 128)
                    orbital = orbital_ref[rows, lanes]
                    applied = first * chosen_ref[0, own, lanes] + second * chosen_ref[1, own, lanes]
                    if step == 0:
                        sums[rows, lanes] = applied
                    else:
                        sums[rows, lanes] = before_ref[rows, lanes] + applied
                    if group == 0:
                        totals[0, own, lanes] = first * orbital
                        totals[1, own, lanes] = second * orbital
                    else:
                        totals[0, own, lanes] += first * orbital
                        totals[1, own, lanes] += second * orbital
        return carry

    lax.fori_loop(0, PAIR // 8, tile, 0)
    core = here_ref[1]
    for offset in range(0, MIDDLE, LANES):
        for where, target in ((core, kept_ref), (1 - core, sent_ref)):
            lanes = pl.ds(pl.multiple_of(where * MIDDLE + offset, 128), LANES)
            first = totals[0, :PLANES, lanes] + totals[0, PLANES:, lanes]
            second = totals[1, :PLANES, lanes] + totals[1, PLANES:, lanes]
            target[:, offset : offset + LANES] = jnp.concatenate([first, second], axis=0)
    if step:
        for block in range(BLOCKS):
            lanes = pl.ds(block * LANES, LANES)
            for band in range(BLOC):
                applied_ref[:, band, lanes] = sums[band * PLANES : band * PLANES + PLANES, lanes]


def pick_kernel(here_ref, owner_ref, picks_ref, orbital_ref, flat_ref, kept_ref, sent_ref):
    core = here_ref[1]
    for offset in range(0, POINTS, LANES):
        lanes = pl.ds(offset, LANES)
        for band in range(BLOC):
            flat_ref[band * PLANES : band * PLANES + PLANES, lanes] = orbital_ref[:, band, lanes]
    for step in range(STEPS):
        mine = owner_ref[step] == here_ref[0]
        for offset in range(0, MIDDLE, LANES):
            for where, target in ((core, kept_ref), (1 - core, sent_ref)):
                lanes = pl.ds(pl.multiple_of(where * MIDDLE + offset, 128), LANES)
                bands = [flat_ref[band * PLANES : band * PLANES + PLANES, lanes] for band in range(BLOC)]
                pair = [pick(bands, picks_ref[step, a]) for a in range(2)]
                target[step * PAIR : step * PAIR + PAIR, offset : offset + LANES] = jnp.where(mine, jnp.concatenate(pair, axis=0), 0.0)


def place_kernel(here_ref, own_ref, other_ref, out_ref):
    core = here_ref[1]
    for step in range(STEPS):
        for offset in range(0, MIDDLE, LANES):
            for where, source in ((core, own_ref), (1 - core, other_ref)):
                lanes = pl.ds(pl.multiple_of(where * MIDDLE + offset, 128), LANES)
                for a in range(2):
                    first = (step * 2 + a) * PLANES
                    out_ref[step, :, a, lanes] = source[first : first + PLANES, offset : offset + LANES]


PARAMS = dict(compiler_params=pltpu.CompilerParams(vmem_limit_bytes=48 * 1024 * 1024))
VMEM = pl.BlockSpec(memory_space=pltpu.VMEM)
SMEM = pl.BlockSpec(memory_space=pltpu.SMEM)
HBM = pl.BlockSpec(memory_space=pltpu.HBM)


def cost(operations, size):
    return pl.CostEstimate(flops=operations, bytes_accessed=size, transcendentals=0)


BOTH_SHAPE = jax.ShapeDtypeStruct((STEPS * PAIR, MIDDLE), jnp.float32)
HALF_SHAPE = jax.ShapeDtypeStruct((PAIR, MIDDLE), jnp.float32)


def pick_orbitals(here, owner, picks, orbitals):
    return pl.pallas_call(
        pick_kernel,
        out_shape=(jax.ShapeDtypeStruct((ROWS, POINTS), jnp.float32),) + (BOTH_SHAPE,) * 2,
        in_specs=[SMEM] * 3 + [VMEM],
        out_specs=(VMEM,) * 3,
        cost_estimate=cost(0, 4_000_000),
        **PARAMS,
    )(here, owner, picks, orbitals)


def place(here, own, other):
    return pl.pallas_call(
        place_kernel,
        out_shape=jax.ShapeDtypeStruct((STEPS, PLANES, 2, POINTS), jnp.float32),
        in_specs=[SMEM] + [VMEM] * 2,
        out_specs=VMEM,
        cost_estimate=cost(0, 2_000_000),
        **PARAMS,
    )(here, own, other)


TABLE_SCRATCH = [
    pltpu.VMEM((2 * LANES, 2 * LANES), jnp.bfloat16),
    pltpu.VMEM((2 * LANES, 2 * LANES), jnp.bfloat16),
    pltpu.SemaphoreType.DMA((2,)),
]


PIECE = jax.ShapeDtypeStruct((ROWS, COLUMNS), jnp.float32)
WHOLE = jax.ShapeDtypeStruct((SLABS, ROWS, COLUMNS), jnp.float32)
STAGED = pltpu.VMEM((SLABS, ROWS, COLUMNS), jnp.float32)


def to_columns(here, orbitals, half, other, step, whole):
    shapes = (WHOLE,) if whole else (PIECE,) * SLABS
    forward, _, twiddle, _ = tables()
    tall = BLOCKS * ROWS
    *columns, chosen = pl.pallas_call(
        functools.partial(forward_kernel, step, whole),
        out_shape=shapes + (jax.ShapeDtypeStruct((2, PAIR, POINTS), jnp.float32),),
        in_specs=[SMEM] + [VMEM] * 5 + [HBM] * 2,
        out_specs=(VMEM,) * (len(shapes) + 1),
        scratch_shapes=[
            pltpu.VMEM((tall, 2 * LANES), jnp.float32),
            pltpu.VMEM((tall, 2 * LANES), jnp.bfloat16),
            pltpu.VMEM((tall, 2 * LANES), jnp.bfloat16),
            STAGED,
        ]
        + TABLE_SCRATCH,
        cost_estimate=cost(6 * tall * (2 * LANES) ** 2, 4_000_000),
        **PARAMS,
    )(here, orbitals, half, other, *twiddle, *forward)
    return columns, chosen


def screened(here, values, kernel):
    _, _, _, along_z = tables()
    whole = len(values) == 1
    shapes = (WHOLE,) if whole else (PIECE,) * SLABS
    return pl.pallas_call(
        functools.partial(middle_kernel, whole),
        out_shape=shapes,
        in_specs=[SMEM] + [VMEM] * (len(values) + 2),
        out_specs=(VMEM,) * len(shapes),
        scratch_shapes=[STAGED],
        cost_estimate=cost(2 * 4 * 4 * NZ * 6 * NZ * COLUMNS, 4_000_000),
        **PARAMS,
    )(here, *values, kernel, along_z)


def from_columns(here, values, orbitals, chosen, step, before=None):
    _, inverse, twiddle, _ = tables()
    tall = BLOCKS * ROWS
    first_step = before is None
    applied = (ROWS, POINTS) if first_step else (PLANES, BLOC, POINTS)
    return pl.pallas_call(
        functools.partial(inverse_kernel, step, len(values) == 1),
        out_shape=(jax.ShapeDtypeStruct(applied, jnp.float32), HALF_SHAPE, HALF_SHAPE),
        in_specs=[SMEM] + [VMEM] * 4 + [HBM] * 2 + [VMEM] * (len(values) + (0 if first_step else 1)),
        out_specs=(VMEM,) * 3,
        scratch_shapes=[
            pltpu.VMEM((tall, 2 * LANES), jnp.bfloat16),
            pltpu.VMEM((tall, 2 * LANES), jnp.bfloat16),
            pltpu.VMEM((tall, 2 * LANES), jnp.float32),
            pltpu.VMEM((2, PAIR, POINTS), jnp.float32),
            STAGED,
        ]
        + TABLE_SCRATCH
        + ([] if first_step else [pltpu.VMEM((ROWS, POINTS), jnp.float32)]),
        cost_estimate=cost(6 * tall * (2 * LANES) ** 2, 8_000_000),
        **PARAMS,
    )(here, orbitals, chosen, *twiddle, *inverse, *values, *(() if first_step else (before,)))


def exchange(pieces):
    if len(pieces) == 1:
        return [lax.all_to_all(pieces[0], ("xh", "y"), split_axis=0, concat_axis=0, tiled=True)]
    moved = [pieces[0]]
    for piece in range(1, SLABS):
        pairs = [
            (x * 4 + y, (x ^ (piece // 4)) * 4 + (y + piece % 4) % 4) for x in range(2) for y in range(4)
        ]
        moved.append(lax.ppermute(pieces[piece], ("xh", "y"), pairs))
    return moved


def per_device(orbitals, owner, picks):
    core, xh, y = lax.axis_index("c"), lax.axis_index("xh"), lax.axis_index("y")
    group = (lax.axis_index("z") * 2 + lax.axis_index("xl")) * 2 + core
    here = jnp.stack([group, core, xh, y]).astype(jnp.int32)
    flat, kept, sent = pick_orbitals(here, owner, picks, orbitals.transpose(1, 0, 2))
    half = spread_near(join_far(join_near(join_cores(kept, sent))))
    other = swap(half, "c", 1)
    columns0, chosen0 = to_columns(here, flat, half, other, 0, True)
    forward0 = exchange(columns0)
    half, _ = tie(half, chosen0)
    columns1, chosen1 = to_columns(here, flat, half, other, 1, True)
    first, xh, y = tie(columns1[0], xh, y)
    kernel = kernel_columns(xh, y)
    forward1 = exchange([first] + columns1[1:])
    backward0 = exchange(screened(here, forward0, kernel))
    backward1 = exchange(screened(here, forward1, kernel))
    applied, kept, sent = from_columns(here, backward0, flat, chosen0, 0)
    part = join_near(join_cores(kept, sent))
    last, part = tie(backward1[0], part)
    applied, kept, sent = from_columns(here, [last] + backward1[1:], flat, chosen1, 1, applied)
    part = jnp.concatenate([part, join_near(join_cores(kept, sent))], axis=0)
    half = spread_near(join_far(part))
    other = swap(half, "c", 1)
    return applied.transpose(1, 0, 2), place(here, half, other).transpose(0, 2, 1, 3)


def solution(mesh):
    fine = Mesh(mesh.devices.reshape(8, 2, 2, 2, 4), ("z", "xl", "c", "xh", "y"))
    band, slab = ("z", "xl", "c"), ("xh", "y")
    in_specs = (P(band, slab, None), P(), P())
    out_specs = (P(band, slab, None), P(None, None, slab, None))
    return jax.shard_map(
        per_device, mesh=fine, in_specs=in_specs, out_specs=out_specs, check_vma=False
    )
```
